32 devices in a mesh: group: 4 (over z), dp: 2 (over y), mp: 4 (over x, core).
Axes of the slice: x: 2, y: 2, z: 4, core: 2. Of those that a mesh axis runs over, the one named last changes fastest.
Arguments:
- image_feats: bfloat16 [48, 1280], P(('group', 'dp')), may hold values from -6 to 6
- image_proj: bfloat16 [1280, 1024], P(None, 'mp'), may hold values from -0.15625 to 0.15625
- tokens: bfloat16 [3, 16, 196, 768], P(None, ('group', 'dp')), may hold values from -6 to 6
- counts: int32 [3, 16], P(None, ('group', 'dp')), may hold values from 50 to 196
- pairing: int32 [3, 16], P(None, ('group', 'dp')), may hold values from 0 to 47, as said below
- w_up: bfloat16 [3, 768, 3072], P(None, None, 'mp'), may hold values from -0.21875 to 0.21875
- w_down: bfloat16 [3, 768, 3072], P(None, None, 'mp'), may hold values from -0.109375 to 0.109375
- w_proj: bfloat16 [3, 768, 1024], P(None, None, 'mp'), may hold values from -0.21875 to 0.21875
Outputs:
- grad_up: float32 [3, 768, 3072], P(None, ('group', 'dp'), 'mp')
- grad_down: float32 [3, 768, 3072], P(None, ('group', 'dp'), 'mp')
- grad_proj: float32 [3, 768, 1024], P(None, ('group', 'dp'), 'mp')
The draws below stay inside these ranges and needn't reach their ends.
Inputs may be any that keep to these rules, and one draw needn't show every extreme that they name: `pairing`: each of the 48 anchors is paired with exactly one sample of one modality.
All inputs are finite; a program needn't handle non-finite values.
Results may differ from the reference program's by a relative error of at most 0.017.
Values may be sent and summed in bfloat16 or wider, within the bound.
A program may use at most 128 MiB of HBM per device.

```python
import jax
import jax.numpy as jnp
from jax import lax

D = 768
FF = 3072
EMB = 1024
IMG_W = 1280
PATCHES = 196
SAMPLES = 16
ANCHORS = 48


def draw_pairing(key, part):
    key = jax.random.fold_in(key, 7)
    return jax.random.permutation(key, ANCHORS).astype(jnp.int32).reshape(3, SAMPLES)


def touch_ends(array, key, smallest, high):
    index_at = [jax.random.randint(jax.random.fold_in(key, axis), (), 0, length) for axis, length in enumerate(array.shape)]
    longest = array.shape.index(max(array.shape))
    neighbour = index_at[:longest] + [(index_at[longest] + 1) % array.shape[longest]] + index_at[longest + 1:]
    return array.at[tuple(index_at)].set(smallest).at[tuple(neighbour)].set(high)


def with_spikes(entries, stream_key, source, target, parts, factor):
    def block_of(position):
        return (jnp.arange(entries.shape[position]) // (entries.shape[position] // parts)).reshape((-1,) + (1,) * (entries.ndim - 1 - position))

    near = jax.random.permutation(stream_key, parts)[block_of(target)]
    far = (block_of(target) + parts // 2) % parts
    return jnp.where((block_of(source) == near) | (block_of(source) == far), factor * entries, entries)


def shard_levels(key, shape, split, smallest, high):
    def one(axis_at, parts):
        steps = jax.random.uniform(jax.random.fold_in(jax.random.fold_in(key, 6), axis_at), (parts,), jnp.float32, smallest / len(split), high / len(split))
        return jnp.repeat(jnp.exp(steps), shape[axis_at] // parts).reshape((-1,) + (1,) * (len(shape) - axis_at - 1))

    factor_of = one(*split[0])
    for cut in split[1:]:
        factor_of = factor_of * one(*cut)
    return factor_of


def noise(key, dims, scale, reach, split=(), kind=jnp.bfloat16):
    gain = shard_levels(key, dims, split, -0.22, 0.18) if split else 1.0
    array = jax.random.normal(key, dims, jnp.float32) * scale * gain
    return jnp.minimum(jnp.maximum(array, -reach), reach).astype(kind)


def gaussian_with(own_key, extent, scale, bound, cuts, heavy, kind=jnp.bfloat16):
    array = scale * jax.random.normal(own_key, extent, jnp.float32)
    if cuts:
        array = array * shard_levels(own_key, extent, cuts, -0.22, 0.18)
    return jnp.clip(with_spikes(array, jax.random.fold_in(own_key, 3), *heavy), -bound, bound).astype(kind)


def setup_inputs(seed: int = 0) -> dict:
    keys = jax.random.split(jax.random.key(seed), 9)
    image_feats = noise(keys[0], (ANCHORS, IMG_W), 1.0, 6.0, ((0, 8),))
    image_proj = noise(keys[1], (IMG_W, EMB), IMG_W ** -0.5, 0.15625, ((1, 4),))
    tokens = gaussian_with(keys[2], (3, SAMPLES, PATCHES, D), 1.0, 6.0, ((1, 8),), (1, 3, 8, 2.0))
    counts = touch_ends(jax.random.randint(keys[3], (3, SAMPLES), PATCHES // 4 + 1, PATCHES + 1), jax.random.fold_in(keys[3], 1), PATCHES // 4 + 1, PATCHES).astype(jnp.int32)
    pairing = draw_pairing(jax.random.fold_in(keys[8], 71), 0)
    w_up = noise(keys[5], (3, D, FF), D ** -0.5, 0.21875, ((2, 4),))
    w_down = noise(keys[6], (3, D, FF), FF ** -0.5, 0.109375, ((2, 4),))
    w_proj = noise(keys[7], (3, D, EMB), D ** -0.5, 0.21875, ((2, 4),))
    return dict(image_feats=image_feats, image_proj=image_proj, tokens=tokens, counts=counts, pairing=pairing, w_up=w_up, w_down=w_down, w_proj=w_proj)


inverse_temp = 14.285714285714286
norm_eps = 1e-05
unit_eps = 1e-06
root_half = 0.7071067811865476
gauss_coef = 0.3989422804014327

def normalize_rows(values):
    centre = lax.optimization_barrier(jnp.mean(values, axis=-1, keepdims=True))
    spread = lax.optimization_barrier(jnp.mean(jnp.square(values - centre), axis=-1, keepdims=True))
    scale_inv = lax.rsqrt(spread + norm_eps)
    return ((values - centre) * scale_inv, scale_inv)

def gelu_value(values):
    return 0.5 * values * (1.0 + lax.erf(values * root_half))

def gelu_slope(values):
    return 0.5 * (1.0 + lax.erf(values * root_half)) + values * jnp.exp(-0.5 * values * values) * gauss_coef

def reference(image_feats, image_proj, tokens, counts, pairing, w_up, w_down, w_proj):
    image_normed = normalize_rows(image_feats.astype(jnp.float32))[0].astype(jnp.bfloat16)
    image_embed = jnp.dot(image_normed, image_proj, preferred_element_type=jnp.float32)
    anchors = (image_embed * lax.rsqrt(lax.optimization_barrier(jnp.sum(image_embed * image_embed, axis=-1, keepdims=True)) + unit_eps)).astype(jnp.bfloat16)
    positions = jnp.arange(PATCHES, dtype=jnp.int32)
    grads_up = []
    grads_down = []
    grads_proj = []
    for modality in range(3):
        samples = tokens[modality]
        normed = normalize_rows(samples.astype(jnp.float32))[0].astype(jnp.bfloat16)
        flat_normed = normed.reshape(-1, D)
        pre_act = jnp.dot(flat_normed, w_up[modality], preferred_element_type=jnp.float32).reshape(SAMPLES, PATCHES, FF)
        lengths = counts[modality]
        weight = jnp.where(positions[None, :] < lengths[:, None], 1.0 / lengths[:, None].astype(jnp.float32), 0.0).astype(jnp.float32)
        act_pool = jnp.einsum('sp,spf->sf', weight, gelu_value(pre_act)).astype(jnp.bfloat16)
        token_pool = jnp.einsum('sp,spd->sd', weight, samples.astype(jnp.float32))
        pooled = token_pool + jnp.dot(act_pool, w_down[modality].T, preferred_element_type=jnp.float32)
        feat_norm, scale_inv = normalize_rows(pooled)
        feat = feat_norm.astype(jnp.bfloat16)
        embedded = jnp.dot(feat, w_proj[modality], preferred_element_type=jnp.float32)
        inv_norm = lax.rsqrt(lax.optimization_barrier(jnp.sum(embedded * embedded, axis=-1, keepdims=True)) + unit_eps)
        unit_rows = embedded * inv_norm
        unit_bf = unit_rows.astype(jnp.bfloat16)
        logits = inverse_temp * jnp.dot(unit_bf, anchors.T, preferred_element_type=jnp.float32)
        exp_logits = jnp.exp(logits)
        prob_bf = (exp_logits / lax.optimization_barrier(jnp.sum(exp_logits, axis=-1, keepdims=True))).astype(jnp.bfloat16)
        weighted = jnp.dot(prob_bf, anchors, preferred_element_type=jnp.float32)
        target = anchors[pairing[modality]].astype(jnp.float32)
        d_unit = inverse_temp * (weighted - target)
        d_embed = ((d_unit - unit_rows * lax.optimization_barrier(jnp.sum(unit_rows * d_unit, axis=-1, keepdims=True))) * inv_norm).astype(jnp.bfloat16)
        grads_proj.append(jnp.dot(feat.T, d_embed, preferred_element_type=jnp.float32))
        d_feat = jnp.dot(d_embed, w_proj[modality].T, preferred_element_type=jnp.float32)
        d_pooled = (scale_inv * (d_feat - lax.optimization_barrier(jnp.mean(d_feat, axis=-1, keepdims=True)) - feat_norm * lax.optimization_barrier(jnp.mean(d_feat * feat_norm, axis=-1, keepdims=True)))).astype(jnp.bfloat16)
        grads_down.append(jnp.dot(d_pooled.T, act_pool, preferred_element_type=jnp.float32))
        d_act = jnp.dot(d_pooled, w_down[modality], preferred_element_type=jnp.float32)
        d_pre = (weight[:, :, None] * d_act[:, None, :] * gelu_slope(pre_act)).astype(jnp.bfloat16)
        grads_up.append(jnp.dot(flat_normed.T, d_pre.reshape(-1, FF), preferred_element_type=jnp.float32))
    return (jnp.stack(grads_up), jnp.stack(grads_down), jnp.stack(grads_proj))
```

```python
import functools

import jax
import jax.numpy as jnp
from jax import lax
from jax.experimental import pallas as pl
from jax.experimental.pallas import tpu as pltpu
from jax.sharding import PartitionSpec as P

MESH = pl.DeviceIdType.MESH
inverse_temp = 14.285714285714286
norm_eps = 1e-05
unit_eps = 1e-06
root_half = 0.7071067811865476
gauss_coef = 0.3989422804014327


def normalize_rows(values):
    centre = jnp.mean(values, axis=-1, keepdims=True)
    spread = jnp.mean(jnp.square(values - centre), axis=-1, keepdims=True)
    scale_inv = lax.rsqrt(spread + norm_eps)
    return ((values - centre) * scale_inv, scale_inv)


def gelu_value(values):
    return 0.5 * values * (1.0 + lax.erf(values * root_half))


def gelu_slope(values):
    return (
        0.5 * (1.0 + lax.erf(values * root_half))
        + values * jnp.exp(-0.5 * values * values) * gauss_coef
    )


def plain_body(image_feats, image_proj, tokens, counts, pairing, w_up, w_down, w_proj):
    image_normed = normalize_rows(image_feats.astype(jnp.float32))[0].astype(jnp.bfloat16)
    embed_cols = jnp.dot(image_normed, image_proj, preferred_element_type=jnp.float32)
    anchor_sq = lax.psum(jnp.sum(embed_cols * embed_cols, axis=-1), "mp")
    anchor_cols = (embed_cols * lax.rsqrt(anchor_sq + unit_eps)[:, None]).astype(jnp.bfloat16)
    num_samples = tokens.shape[1]
    num_patches = tokens.shape[2]
    feature_width = tokens.shape[3]
    positions = jnp.arange(num_patches, dtype=jnp.int32)
    inside = positions[None, None, :] < counts[:, :, None]
    weight = jnp.where(inside, 1.0 / counts[:, :, None].astype(jnp.float32), 0.0)
    mask_bf = inside.astype(jnp.bfloat16)
    normed_list = []
    pre_list = []
    pool_list = []
    partials = []
    for modality in range(3):
        normed = (
            normalize_rows(tokens[modality].astype(jnp.float32))[0]
            .astype(jnp.bfloat16)
            .reshape(-1, feature_width)
        )
        pre_act = jnp.dot(normed, w_up[modality], preferred_element_type=jnp.float32).reshape(
            num_samples, num_patches, -1
        )
        act_pool = jnp.einsum("sp,spf->sf", weight[modality], gelu_value(pre_act)).astype(
            jnp.bfloat16
        )
        partials.append(
            lax.dot_general(
                act_pool,
                w_down[modality],
                (((1,), (1,)), ((), ())),
                preferred_element_type=jnp.float32,
            )
        )
        normed_list.append(normed)
        pre_list.append(pre_act)
        pool_list.append(act_pool)
    token_pool = jnp.einsum(
        "msp,mspd->msd", mask_bf, tokens, preferred_element_type=jnp.float32
    ) / counts[:, :, None].astype(jnp.float32)
    pooled = token_pool + lax.psum(jnp.stack(partials), "mp")
    feat_norm, scale_inv = normalize_rows(pooled)
    feat = feat_norm.astype(jnp.bfloat16)
    embedded = jnp.einsum("msd,mde->mse", feat, w_proj, preferred_element_type=jnp.float32)
    embed_sq = lax.psum(jnp.sum(embedded * embedded, axis=-1), "mp")
    inv_norm = lax.rsqrt(embed_sq + unit_eps)[..., None]
    unit_rows = embedded * inv_norm
    queries = unit_rows.astype(jnp.bfloat16).reshape(3 * num_samples, -1)
    target_rows = pairing.reshape(-1)
    own_table = lax.all_gather(anchor_cols, ("group", "dp"), axis=0, tiled=True)
    part_logits = jnp.dot(queries, own_table.T, preferred_element_type=jnp.float32)
    logits = inverse_temp * lax.psum(part_logits, "mp")
    exp_logits = jnp.exp(logits)
    prob_bf = (exp_logits / jnp.sum(exp_logits, axis=-1, keepdims=True)).astype(jnp.bfloat16)
    weighted = jnp.dot(prob_bf, own_table, preferred_element_type=jnp.float32)
    target = jnp.take(own_table, target_rows, axis=0).astype(jnp.float32)
    d_unit = (inverse_temp * (weighted - target)).reshape(unit_rows.shape)
    unit_dots = lax.psum(jnp.sum(unit_rows * d_unit, axis=-1), "mp")
    d_embed = ((d_unit - unit_rows * unit_dots[..., None]) * inv_norm).astype(jnp.bfloat16)
    d_feat = lax.psum(
        jnp.einsum("mse,mde->msd", d_embed, w_proj, preferred_element_type=jnp.float32), "mp"
    )
    d_pooled = (
        scale_inv
        * (
            d_feat
            - jnp.mean(d_feat, axis=-1, keepdims=True)
            - feat_norm * jnp.mean(d_feat * feat_norm, axis=-1, keepdims=True)
        )
    ).astype(jnp.bfloat16)
    pool_stack = jnp.stack(pool_list)
    feat_all, dpool_all, act_all, dembed_all = (
        lax.all_gather(feat, ("group", "dp"), axis=1, tiled=True),
        lax.all_gather(d_pooled, ("group", "dp"), axis=1, tiled=True),
        lax.all_gather(pool_stack, ("group", "dp"), axis=1, tiled=True),
        lax.all_gather(d_embed, ("group", "dp"), axis=1, tiled=True),
    )
    row_count = feature_width // lax.axis_size(("group", "dp"))
    row_start = lax.axis_index(("group", "dp")) * row_count
    feat_rows = lax.dynamic_slice_in_dim(feat_all, row_start, row_count, 2)
    dpool_rows = lax.dynamic_slice_in_dim(dpool_all, row_start, row_count, 2)
    down_shards = jnp.einsum(
        "msd,msf->mdf", dpool_rows, act_all, preferred_element_type=jnp.float32
    )
    proj_shards = jnp.einsum(
        "msd,mse->mde", feat_rows, dembed_all, preferred_element_type=jnp.float32
    )
    joined_list = []
    for modality in range(3):
        d_act = jnp.dot(d_pooled[modality], w_down[modality], preferred_element_type=jnp.float32)
        d_pre = (
            weight[modality][:, :, None] * d_act[:, None, :] * gelu_slope(pre_list[modality])
        ).astype(jnp.bfloat16)
        grad_up = lax.dot_general(
            normed_list[modality],
            d_pre.reshape(-1, d_pre.shape[2]),
            (((0,), (0,)), ((), ())),
            preferred_element_type=jnp.float32,
        )
        joined_list.append(grad_up)
    stacked = jnp.stack(joined_list)
    stacked = lax.psum_scatter(stacked, ("group", "dp"), scatter_dimension=1, tiled=True)
    return (stacked, down_shards, proj_shards)

def fwd_kernel(counts_ref, tok_ref, up_ref, h_ref, act_ref, pool_ref):
    m, s = pl.program_id(0), pl.program_id(1)
    per = pl.num_programs(1)
    row = m * per + s

    @pl.when(row == 0)
    def _():
        act_ref[...] = jnp.zeros_like(act_ref)
        pool_ref[...] = jnp.zeros_like(pool_ref)

    count = counts_ref[m, s]
    x = tok_ref[0, 0].astype(jnp.float32)
    normed = normalize_rows(x)[0].astype(jnp.bfloat16)
    inv = 1.0 / jnp.full((x.shape[0], 1), count, jnp.int32).astype(jnp.float32)
    index = lax.broadcasted_iota(jnp.int32, (x.shape[0], 1), 0)
    weight = jnp.where(index < count, inv, 0.0)
    pre = jnp.dot(normed, up_ref[0], preferred_element_type=jnp.float32)
    phi = 0.5 * (1.0 + lax.erf(pre * root_half))
    slope = phi + pre * jnp.exp(-0.5 * pre * pre) * gauss_coef
    act_ref[pl.ds(row, 1), :] = jnp.sum(weight * (pre * phi), axis=0, keepdims=True)
    pool_ref[pl.ds(row, 1), :] = jnp.sum(weight * x, axis=0, keepdims=True)
    sloped = (weight * slope).astype(jnp.bfloat16)
    h_ref[0] = lax.dot_general(
        normed, sloped, (((0,), (0,)), ((), ())), preferred_element_type=jnp.float32
    ).astype(jnp.bfloat16)


def peer_of(r, ndp):
    return {"group": r // ndp, "dp": lax.rem(r, ndp)}


def mid_kernel(
    sizes, pair_ref, img_ref, iproj_ref, act_ref, pool_ref, down_ref, proj_ref,
    dact_ref, gdown_ref, gproj_ref,
    e_slots, sq_slots, p_slots, l_slots, f_slots, ga, gb, gt,
    e_ss, e_rs, sq_ss, sq_rs, p_ss, p_rs, l_ss, l_rs, f_ss, f_rs, a_ss, a_rs, b_ss, b_rs,
):
    ngroup, ndp, nmp, per, apd = sizes
    nr = ngroup * ndp
    r = lax.axis_index("group") * ndp + lax.axis_index("dp")
    me = lax.axis_index("mp")
    nmod = down_ref.shape[0]
    rows = act_ref.shape[0]
    barrier = pltpu.get_barrier_semaphore()
    for k in range(1, nmp):
        pl.semaphore_signal(barrier, inc=1, device_id={"mp": lax.rem(me + k, nmp)}, device_id_type=MESH)
    for k in range(1, nr):
        pl.semaphore_signal(barrier, inc=1, device_id=peer_of(lax.rem(r + k, nr), ndp), device_id_type=MESH)
    pl.semaphore_wait(barrier, nmp - 1 + nr - 1)

    def spread(slots, ss, rs, across_mp):
        slot = me if across_mp else r
        out = []
        for k in range(1, nmp if across_mp else nr):
            device = {"mp": lax.rem(me + k, nmp)} if across_mp else peer_of(lax.rem(r + k, nr), ndp)
            copy = pltpu.make_async_remote_copy(
                src_ref=slots.at[slot], dst_ref=slots.at[slot],
                send_sem=ss.at[k - 1], recv_sem=rs.at[k - 1],
                device_id=device, device_id_type=MESH,
            )
            copy.start()
            out.append(copy)
        return out

    def arrive(copies):
        for copy in copies:
            copy.wait_recv()

    started = []
    row_id = lax.broadcasted_iota(jnp.int32, (rows, 1), 0)
    of_mod = [(row_id >= m * per) & (row_id < (m + 1) * per) for m in range(nmod)]

    def by_mod(values, w_ref, dim):
        total = None
        for m in range(nmod):
            part = lax.dot_general(
                jnp.where(of_mod[m], values, 0.0).astype(jnp.bfloat16), w_ref[m],
                (((1,), (dim,)), ((), ())), preferred_element_type=jnp.float32,
            )
            total = part if total is None else total + part
        return total

    act = act_ref[...].astype(jnp.bfloat16).astype(jnp.float32)
    p_slots[me] = by_mod(act, down_ref, 1)
    pooled_copies = spread(p_slots, p_ss, p_rs, True)
    image = normalize_rows(img_ref[...].astype(jnp.float32))[0].astype(jnp.bfloat16)
    e_slots[r] = jnp.dot(image, iproj_ref[...], preferred_element_type=jnp.float32)
    e_copies = spread(e_slots, e_ss, e_rs, False)
    arrive(e_copies)
    embed = e_slots[...].reshape(nr * 8, -1)
    square = jnp.sum(embed * embed, axis=-1, keepdims=True)
    sq_slots[me] = jnp.broadcast_to(square, sq_slots.shape[1:])
    sq_copies = spread(sq_slots, sq_ss, sq_rs, True)

    arrive(pooled_copies)
    pooled = pool_ref[...]
    for k in range(nmp):
        pooled = pooled + p_slots[k]
    feat_norm, scale_inv = normalize_rows(pooled)
    ga[r] = jnp.concatenate([act, feat_norm], axis=0).astype(jnp.bfloat16)
    a_copies = spread(ga, a_ss, a_rs, False)
    embedded = by_mod(feat_norm, proj_ref, 0)
    own_sq = jnp.sum(embedded * embedded, axis=-1, keepdims=True)

    arrive(sq_copies)
    square = sq_slots[0]
    for k in range(1, nmp):
        square = square + sq_slots[k]
    anchors = (embed * lax.rsqrt(square[:, :1] + unit_eps)).astype(jnp.bfloat16)
    table = jnp.concatenate([anchors, jnp.zeros((128 - nr * 8, anchors.shape[1]), jnp.bfloat16)], axis=0)
    part = lax.dot_general(
        embedded.astype(jnp.bfloat16), table, (((1,), (1,)), ((), ())),
        preferred_element_type=jnp.float32,
    )
    col = lax.broadcasted_iota(jnp.int32, (rows, 128), 1)
    l_slots[me] = jnp.where(col < nr * 8, part, own_sq)
    l_copies = spread(l_slots, l_ss, l_rs, True)
    hot = jnp.zeros((rows, 128), jnp.float32)
    anchor_of = (col // 8) * apd + col % 8
    valid = (col % 8 < apd) & (col < nr * 8)
    for m in range(nmod):
        for s in range(per):
            hit = valid & (anchor_of == pair_ref[m, s]) & (row_id == m * per + s)
            hot = jnp.where(hit, 1.0, hot)
    arrive(l_copies)
    both = l_slots[0]
    for k in range(1, nmp):
        both = both + l_slots[k]
    inv_norm = lax.rsqrt(both[:, 127:] + unit_eps)
    logits = inverse_temp * (both * inv_norm)
    expl = jnp.where(valid, jnp.exp(jnp.where(valid, logits, 0.0)), 0.0)
    prob = (expl / jnp.sum(expl, axis=-1, keepdims=True)).astype(jnp.bfloat16)
    dots = jnp.sum(
        jnp.where(valid, (prob.astype(jnp.float32) - hot) * logits, 0.0), axis=-1, keepdims=True
    )
    weighted = jnp.dot(prob, table, preferred_element_type=jnp.float32)
    target = jnp.dot(hot.astype(jnp.bfloat16), table, preferred_element_type=jnp.float32)
    d_unit = inverse_temp * (weighted - target)
    d_embed = ((d_unit - embedded * inv_norm * dots) * inv_norm).astype(jnp.bfloat16).astype(jnp.float32)
    f_slots[me] = by_mod(d_embed, proj_ref, 1)
    f_copies = spread(f_slots, f_ss, f_rs, True)
    arrive(f_copies)
    d_feat = f_slots[0]
    for k in range(1, nmp):
        d_feat = d_feat + f_slots[k]
    d_pooled = scale_inv * (
        d_feat
        - jnp.mean(d_feat, axis=-1, keepdims=True)
        - feat_norm * jnp.mean(d_feat * feat_norm, axis=-1, keepdims=True)
    )
    wide = jnp.concatenate([d_embed, jnp.zeros((rows, ga.shape[2] - d_embed.shape[1]), jnp.float32)], axis=1)
    gb[r] = jnp.concatenate([d_pooled, wide], axis=0).astype(jnp.bfloat16)
    b_copies = spread(gb, b_ss, b_rs, False)
    dact_ref[...] = by_mod(d_pooled, down_ref, 0)
    arrive(a_copies)
    arrive(b_copies)

    all_a = ga[...].reshape(nr * 16, -1)
    all_b = gb[...].reshape(nr * 16, -1)
    height = gdown_ref.shape[1]
    mine = pl.ds(pl.multiple_of(r * height, height), height)
    lane = lax.broadcasted_iota(jnp.int32, (1, nr * 16), 1) % 16
    width = gproj_ref.shape[2]
    gt[...] = all_b.astype(jnp.float32).T
    lhs = gt[mine, :]
    for m in range(nmod):
        keep = (lane >= m * per) & (lane < (m + 1) * per)
        gdown_ref[m] = jnp.dot(
            jnp.where(keep, lhs, 0.0).astype(jnp.bfloat16), all_a, preferred_element_type=jnp.float32
        )
    gt[...] = all_a.astype(jnp.float32).T
    lhs = gt[mine, :]
    for m in range(nmod):
        keep = (lane >= 8 + m * per) & (lane < 8 + (m + 1) * per)
        gproj_ref[m] = jnp.dot(
            jnp.where(keep, lhs, 0.0).astype(jnp.bfloat16), all_b[:, :width],
            preferred_element_type=jnp.float32,
        )
    for copy in pooled_copies + e_copies + sq_copies + a_copies + l_copies + f_copies + b_copies:
        copy.wait_send()


def scatter_kernel(
    sizes, h_ref, dact_ref, out_ref, y_send, y_recv, z_send, z_recv, y_ss, y_rs, z_ss, z_rs
):
    ngroup, ndp, nmp, per, apd = sizes
    g, d = lax.axis_index("group"), lax.axis_index("dp")
    nmod, height = out_ref.shape[:2]
    barrier = pltpu.get_barrier_semaphore()
    pl.semaphore_signal(barrier, inc=1, device_id={"dp": 1 - d}, device_id_type=MESH)
    for k in range(1, ngroup):
        pl.semaphore_signal(barrier, inc=1, device_id={"group": lax.rem(g + k, ngroup)}, device_id_type=MESH)
    pl.semaphore_wait(barrier, ngroup)

    def term(m, group, dp):
        at = pl.ds(pl.multiple_of((group * ndp + dp) * height, height), height)
        total = None
        for s in range(per):
            row = m * per + s
            part = h_ref[row, at, :].astype(jnp.float32) * dact_ref[row : row + 1, :]
            total = part if total is None else total + part
        return total

    y_copies, z_copies = [], []
    for m in range(nmod):
        for group in range(ngroup):
            y_send[m, group] = term(m, group, 1 - d).astype(jnp.bfloat16)
        copy = pltpu.make_async_remote_copy(
            src_ref=y_send.at[m], dst_ref=y_recv.at[m], send_sem=y_ss.at[m], recv_sem=y_rs.at[m],
            device_id={"dp": 1 - d}, device_id_type=MESH,
        )
        copy.start()
        y_copies.append(copy)
    for m in range(nmod):
        y_copies[m].wait_recv()
        for k in range(1, ngroup):
            to = lax.rem(g + k, ngroup)
            z_send[m, k - 1] = (term(m, to, d) + y_recv[m, to].astype(jnp.float32)).astype(jnp.bfloat16)
            copy = pltpu.make_async_remote_copy(
                src_ref=z_send.at[m, k - 1], dst_ref=z_recv.at[m, k - 1],
                send_sem=z_ss.at[m, k - 1], recv_sem=z_rs.at[m, k - 1],
                device_id={"group": to}, device_id_type=MESH,
            )
            copy.start()
            z_copies.append(copy)
        out_ref[m] = term(m, g, d) + y_recv[m, g].astype(jnp.float32)
    for m in range(nmod):
        total = out_ref[m]
        for k in range(1, ngroup):
            z_copies[m * (ngroup - 1) + k - 1].wait_recv()
            total = total + z_recv[m, k - 1].astype(jnp.float32)
        out_ref[m] = total
    for copy in y_copies + z_copies:
        copy.wait_send()


def kernel_body(mesh, image_feats, image_proj, tokens, counts, pairing, w_up, w_down, w_proj):
    ngroup, ndp, nmp = mesh.shape["group"], mesh.shape["dp"], mesh.shape["mp"]
    nr = ngroup * ndp
    nmod, per, patches, width = tokens.shape
    hidden, emb = w_up.shape[2], w_proj.shape[2]
    apd = image_feats.shape[0]
    sizes = (ngroup, ndp, nmp, per, apd)
    height = width // nr
    f32, bf16 = jnp.float32, jnp.bfloat16
    vmem = pl.BlockSpec(memory_space=pltpu.VMEM)
    smem = pl.BlockSpec(memory_space=pltpu.SMEM)
    h, act, token_pool = pl.pallas_call(
        fwd_kernel,
        grid=(nmod, per),
        in_specs=[
            smem,
            pl.BlockSpec((1, 1, patches, width), lambda m, s: (m, s, 0, 0)),
            pl.BlockSpec((1, width, hidden), lambda m, s: (m, 0, 0)),
        ],
        out_specs=[
            pl.BlockSpec((1, width, hidden), lambda m, s: (m * per + s, 0, 0)),
            pl.BlockSpec((8, hidden), lambda m, s: (0, 0)),
            pl.BlockSpec((8, width), lambda m, s: (0, 0)),
        ],
        out_shape=[
            jax.ShapeDtypeStruct((nmod * per, width, hidden), bf16),
            jax.ShapeDtypeStruct((8, hidden), f32),
            jax.ShapeDtypeStruct((8, width), f32),
        ],
        compiler_params=pltpu.CompilerParams(vmem_limit_bytes=40 << 20),
        name="forward",
    )(counts, tokens, w_up)
    image = jnp.pad(image_feats, ((0, 8 - apd), (0, 0)))
    sem = pltpu.SemaphoreType.DMA
    d_act, grad_down, grad_proj = pl.pallas_call(
        functools.partial(mid_kernel, sizes),
        in_specs=[smem] + [vmem] * 6,
        out_specs=[vmem] * 3,
        out_shape=[
            jax.ShapeDtypeStruct((8, hidden), f32),
            jax.ShapeDtypeStruct((nmod, height, hidden), f32),
            jax.ShapeDtypeStruct((nmod, height, emb), f32),
        ],
        scratch_shapes=[
            pltpu.VMEM((nr, 8, emb), f32),
            pltpu.VMEM((nmp, nr * 8, 128), f32),
            pltpu.VMEM((nmp, 8, width), f32),
            pltpu.VMEM((nmp, 8, 128), f32),
            pltpu.VMEM((nmp, 8, width), f32),
            pltpu.VMEM((nr, 16, width), bf16),
            pltpu.VMEM((nr, 16, width), bf16),
            pltpu.VMEM((width, nr * 16), f32),
        ]
        + [sem((nr - 1,))] * 2
        + [sem((nmp - 1,))] * 8
        + [sem((nr - 1,))] * 4,
        compiler_params=pltpu.CompilerParams(
            collective_id=0, has_side_effects=True, vmem_limit_bytes=40 << 20
        ),
        name="middle",
    )(pairing, image, image_proj, act, token_pool, w_down, w_proj)
    grad_up = pl.pallas_call(
        functools.partial(scatter_kernel, sizes),
        in_specs=[vmem] * 2,
        out_specs=vmem,
        out_shape=jax.ShapeDtypeStruct((nmod, height, hidden), f32),
        scratch_shapes=[
            pltpu.VMEM((nmod, ngroup, height, hidden), bf16),
            pltpu.VMEM((nmod, ngroup, height, hidden), bf16),
            pltpu.VMEM((nmod, ngroup - 1, height, hidden), bf16),
            pltpu.VMEM((nmod, ngroup - 1, height, hidden), bf16),
            sem((nmod,)),
            sem((nmod,)),
            sem((nmod, ngroup - 1)),
            sem((nmod, ngroup - 1)),
        ],
        compiler_params=pltpu.CompilerParams(
            collective_id=1, has_side_effects=True, vmem_limit_bytes=40 << 20
        ),
        name="scatter",
    )(h, d_act)
    return (grad_up, grad_down, grad_proj)


def solution(mesh):
    in_specs = (
        P(("group", "dp"), None),
        P(None, "mp"),
        P(None, ("group", "dp"), None, None),
        P(None, ("group", "dp")),
        P(None, ("group", "dp")),
        P(None, None, "mp"),
        P(None, None, "mp"),
        P(None, None, "mp"),
    )
    out_specs = (
        P(None, ("group", "dp"), "mp"),
        P(None, ("group", "dp"), "mp"),
        P(None, ("group", "dp"), "mp"),
    )
    devices = mesh.shape["group"] * mesh.shape["dp"]
    fits = devices <= 8 and mesh.shape["dp"] == 2
    body = functools.partial(kernel_body, mesh) if fits else plain_body
    return jax.shard_map(body, mesh=mesh, in_specs=in_specs, out_specs=out_specs, check_vma=False)
```

```python
import functools

import jax
import jax.numpy as jnp
from jax import lax
from jax.experimental import pallas as pl
from jax.experimental.pallas import tpu as pltpu
from jax.sharding import PartitionSpec as P

MESH = pl.DeviceIdType.MESH
inverse_temp = 14.285714285714286
norm_eps = 1e-05
unit_eps = 1e-06
root_half = 0.7071067811865476
gauss_coef = 0.3989422804014327


def normalize_rows(values):
    centre = jnp.mean(values, axis=-1, keepdims=True)
    spread = jnp.mean(jnp.square(values - centre), axis=-1, keepdims=True)
    scale_inv = lax.rsqrt(spread + norm_eps)
    return ((values - centre) * scale_inv, scale_inv)


def gelu_value(values):
    return 0.5 * values * (1.0 + lax.erf(values * root_half))


def gelu_slope(values):
    return (
        0.5 * (1.0 + lax.erf(values * root_half))
        + values * jnp.exp(-0.5 * values * values) * gauss_coef
    )


def plain_body(image_feats, image_proj, tokens, counts, pairing, w_up, w_down, w_proj):
    image_normed = normalize_rows(image_feats.astype(jnp.float32))[0].astype(jnp.bfloat16)
    embed_cols = jnp.dot(image_normed, image_proj, preferred_element_type=jnp.float32)
    anchor_sq = lax.psum(jnp.sum(embed_cols * embed_cols, axis=-1), "mp")
    anchor_cols = (embed_cols * lax.rsqrt(anchor_sq + unit_eps)[:, None]).astype(jnp.bfloat16)
    num_samples = tokens.shape[1]
    num_patches = tokens.shape[2]
    feature_width = tokens.shape[3]
    positions = jnp.arange(num_patches, dtype=jnp.int32)
    inside = positions[None, None, :] < counts[:, :, None]
    weight = jnp.where(inside, 1.0 / counts[:, :, None].astype(jnp.float32), 0.0)
    mask_bf = inside.astype(jnp.bfloat16)
    normed_list = []
    pre_list = []
    pool_list = []
    partials = []
    for modality in range(3):
        normed = (
            normalize_rows(tokens[modality].astype(jnp.float32))[0]
            .astype(jnp.bfloat16)
            .reshape(-1, feature_width)
        )
        pre_act = jnp.dot(normed, w_up[modality], preferred_element_type=jnp.float32).reshape(
            num_samples, num_patches, -1
        )
        act_pool = jnp.einsum("sp,spf->sf", weight[modality], gelu_value(pre_act)).astype(
            jnp.bfloat16
        )
        partials.append(
            lax.dot_general(
                act_pool,
                w_down[modality],
                (((1,), (1,)), ((), ())),
                preferred_element_type=jnp.float32,
            )
        )
        normed_list.append(normed)
        pre_list.append(pre_act)
        pool_list.append(act_pool)
    token_pool = jnp.einsum(
        "msp,mspd->msd", mask_bf, tokens, preferred_element_type=jnp.float32
    ) / counts[:, :, None].astype(jnp.float32)
    pooled = token_pool + lax.psum(jnp.stack(partials), "mp")
    feat_norm, scale_inv = normalize_rows(pooled)
    feat = feat_norm.astype(jnp.bfloat16)
    embedded = jnp.einsum("msd,mde->mse", feat, w_proj, preferred_element_type=jnp.float32)
    embed_sq = lax.psum(jnp.sum(embedded * embedded, axis=-1), "mp")
    inv_norm = lax.rsqrt(embed_sq + unit_eps)[..., None]
    unit_rows = embedded * inv_norm
    queries = unit_rows.astype(jnp.bfloat16).reshape(3 * num_samples, -1)
    target_rows = pairing.reshape(-1)
    own_table = lax.all_gather(anchor_cols, ("group", "dp"), axis=0, tiled=True)
    part_logits = jnp.dot(queries, own_table.T, preferred_element_type=jnp.float32)
    logits = inverse_temp * lax.psum(part_logits, "mp")
    exp_logits = jnp.exp(logits)
    prob_bf = (exp_logits / jnp.sum(exp_logits, axis=-1, keepdims=True)).astype(jnp.bfloat16)
    weighted = jnp.dot(prob_bf, own_table, preferred_element_type=jnp.float32)
    target = jnp.take(own_table, target_rows, axis=0).astype(jnp.float32)
    d_unit = (inverse_temp * (weighted - target)).reshape(unit_rows.shape)
    unit_dots = lax.psum(jnp.sum(unit_rows * d_unit, axis=-1), "mp")
    d_embed = ((d_unit - unit_rows * unit_dots[..., None]) * inv_norm).astype(jnp.bfloat16)
    d_feat = lax.psum(
        jnp.einsum("mse,mde->msd", d_embed, w_proj, preferred_element_type=jnp.float32), "mp"
    )
    d_pooled = (
        scale_inv
        * (
            d_feat
            - jnp.mean(d_feat, axis=-1, keepdims=True)
            - feat_norm * jnp.mean(d_feat * feat_norm, axis=-1, keepdims=True)
        )
    ).astype(jnp.bfloat16)
    pool_stack = jnp.stack(pool_list)
    feat_all, dpool_all, act_all, dembed_all = (
        lax.all_gather(feat, ("group", "dp"), axis=1, tiled=True),
        lax.all_gather(d_pooled, ("group", "dp"), axis=1, tiled=True),
        lax.all_gather(pool_stack, ("group", "dp"), axis=1, tiled=True),
        lax.all_gather(d_embed, ("group", "dp"), axis=1, tiled=True),
    )
    row_count = feature_width // lax.axis_size(("group", "dp"))
    row_start = lax.axis_index(("group", "dp")) * row_count
    feat_rows = lax.dynamic_slice_in_dim(feat_all, row_start, row_count, 2)
    dpool_rows = lax.dynamic_slice_in_dim(dpool_all, row_start, row_count, 2)
    down_shards = jnp.einsum(
        "msd,msf->mdf", dpool_rows, act_all, preferred_element_type=jnp.float32
    )
    proj_shards = jnp.einsum(
        "msd,mse->mde", feat_rows, dembed_all, preferred_element_type=jnp.float32
    )
    joined_list = []
    for modality in range(3):
        d_act = jnp.dot(d_pooled[modality], w_down[modality], preferred_element_type=jnp.float32)
        d_pre = (
            weight[modality][:, :, None] * d_act[:, None, :] * gelu_slope(pre_list[modality])
        ).astype(jnp.bfloat16)
        grad_up = lax.dot_general(
            normed_list[modality],
            d_pre.reshape(-1, d_pre.shape[2]),
            (((0,), (0,)), ((), ())),
            preferred_element_type=jnp.float32,
        )
        joined_list.append(grad_up)
    stacked = jnp.stack(joined_list)
    stacked = lax.psum_scatter(stacked, ("group", "dp"), scatter_dimension=1, tiled=True)
    return (stacked, down_shards, proj_shards)

def peer_of(r, ndp):
    return {"group": r // ndp, "dp": lax.rem(r, ndp)}


def step_kernel(
    sizes, count_ref, pair_ref, img_ref, iproj_ref, tok_ref, up_ref, down_ref, proj_ref,
    gup_ref, gdown_ref, gproj_ref,
    img, normed_of, sloped_of, h, e_slots, sq_slots, p_slots, l_slots, f_slots, ga, gb, gt,
    y_send, y_recv, z_send, z_recv,
    e_ss, e_rs, sq_ss, sq_rs, p_ss, p_rs, l_ss, l_rs, f_ss, f_rs, a_ss, a_rs, b_ss, b_rs,
    y_ss, y_rs, z_ss, z_rs,
):
    ngroup, ndp, nmp, per, apd, cuts = sizes
    nr = ngroup * ndp
    g, d = lax.axis_index("group"), lax.axis_index("dp")
    r = g * ndp + d
    me = lax.axis_index("mp")
    nmod = down_ref.shape[0]
    rows = 8
    f32, bf16 = jnp.float32, jnp.bfloat16
    barrier = pltpu.get_barrier_semaphore()
    for k in range(1, nmp):
        pl.semaphore_signal(barrier, inc=1, device_id={"mp": lax.rem(me + k, nmp)}, device_id_type=MESH)
    for k in range(1, nr):
        pl.semaphore_signal(barrier, inc=1, device_id=peer_of(lax.rem(r + k, nr), ndp), device_id_type=MESH)

    sent = []

    def spread(slots, ss, rs, across_mp, base=0, lead=()):
        slot = me if across_mp else r
        out = []
        for k in range(1, nmp if across_mp else nr):
            device = {"mp": lax.rem(me + k, nmp)} if across_mp else peer_of(lax.rem(r + k, nr), ndp)
            ref = slots.at[lead + (slot,)]
            copy = pltpu.make_async_remote_copy(
                src_ref=ref, dst_ref=ref, send_sem=ss.at[base + k - 1], recv_sem=rs.at[base + k - 1],
                device_id=device, device_id_type=MESH,
            )
            copy.start()
            out.append(copy)
        sent.extend(out)
        return out

    def arrive(copies):
        for copy in copies:
            copy.wait_recv()

    row_id = lax.broadcasted_iota(jnp.int32, (rows, 1), 0)
    col = lax.broadcasted_iota(jnp.int32, (rows, 128), 1)
    anchor_of = (col // 8) * apd + col % 8
    valid = (col % 8 < apd) & (col < nr * 8)

    def matmul(lhs, rhs, left, right):
        return lax.dot_general(
            lhs.astype(bf16), rhs, (((left,), (right,)), ((), ())), preferred_element_type=f32
        )

    act, pool, pooled_copies = [], [], []

    def forward(m):
        act_rows = jnp.zeros((rows, up_ref.shape[2]), f32)
        pool_rows = jnp.zeros((rows, tok_ref.shape[3]), f32)
        for s in range(per):
            row = m * per + s
            x = tok_ref[m, s].astype(f32)
            normed = normalize_rows(x)[0].astype(bf16)
            normed_of[row] = normed
            count = jnp.full((x.shape[0], 1), count_ref[m, s], jnp.int32)
            index = lax.broadcasted_iota(jnp.int32, (x.shape[0], 1), 0)
            weight = jnp.where(index < count, 1.0 / count.astype(f32), 0.0)
            pre = jnp.dot(normed, up_ref[m], preferred_element_type=f32)
            phi = 0.5 * (1.0 + lax.erf(pre * root_half))
            slope = phi + pre * jnp.exp(-0.5 * pre * pre) * gauss_coef
            sloped_of[row] = (weight * slope).astype(bf16)
            here = row_id == row
            act_rows = jnp.where(here, jnp.sum(weight * (pre * phi), axis=0, keepdims=True), act_rows)
            pool_rows = jnp.where(here, jnp.sum(weight * x, axis=0, keepdims=True), pool_rows)
        act_rows = act_rows.astype(bf16).astype(f32)
        act.append(act_rows)
        pool.append(pool_rows)
        p_slots[m, me] = matmul(act_rows, down_ref[m], 1, 1)
        pooled_copies.append(spread(p_slots, p_ss, p_rs, True, m * (nmp - 1), (m,)))

    feat, scale, embeds, logit_copies = [], [], [], []

    def total_of(slots, m):
        total = slots[m, 0]
        for k in range(1, nmp):
            total = total + slots[m, k]
        return total

    def score(m, table):
        arrive(pooled_copies[m])
        feat_norm, scale_inv = normalize_rows(pool[m] + total_of(p_slots, m))
        feat.append(feat_norm)
        scale.append(scale_inv)
        embedded = matmul(feat_norm, proj_ref[m], 1, 0)
        embeds.append(embedded)
        own_sq = jnp.sum(embedded * embedded, axis=-1, keepdims=True)
        part = matmul(embedded, table, 1, 1)
        l_slots[m, me] = jnp.where(col < nr * 8, part, own_sq)
        logit_copies.append(spread(l_slots, l_ss, l_rs, True, m * (nmp - 1), (m,)))

    d_embeds, feat_copies = [], []

    def loss_slope(m, table):
        hot = jnp.zeros((rows, 128), f32)
        for s in range(per):
            hot = jnp.where(valid & (anchor_of == pair_ref[m, s]) & (row_id == m * per + s), 1.0, hot)
        arrive(logit_copies[m])
        both = total_of(l_slots, m)
        inv_norm = lax.rsqrt(both[:, 127:] + unit_eps)
        logits = jnp.where(valid, inverse_temp * (both * inv_norm), 0.0)
        expl = jnp.where(valid, jnp.exp(logits), 0.0)
        prob = (expl / jnp.sum(expl, axis=-1, keepdims=True)).astype(bf16)
        dots = jnp.sum((prob.astype(f32) - hot) * logits, axis=-1, keepdims=True)
        d_unit = inverse_temp * (matmul(prob, table, 1, 0) - matmul(hot, table, 1, 0))
        d_embed = (d_unit - embeds[m] * inv_norm * dots) * inv_norm
        own = (row_id >= m * per) & (row_id < (m + 1) * per)
        d_embed = jnp.where(own, d_embed, 0.0).astype(bf16).astype(f32)
        d_embeds.append(d_embed)
        f_slots[m, me] = matmul(d_embed, proj_ref[m], 1, 1)
        feat_copies.append(spread(f_slots, f_ss, f_rs, True, m * (nmp - 1), (m,)))

    def products(m):
        for s in range(per):
            row = m * per + s
            h[row] = lax.dot_general(
                normed_of[row], sloped_of[row], (((0,), (0,)), ((), ())), preferred_element_type=f32
            ).astype(bf16)

    d_pools, d_acts, y_copies, z_copies = [], [], [], []
    height, hidden = gup_ref.shape[1:]
    width = hidden // cuts

    def term(m, cut, group, dp):
        at = pl.ds(pl.multiple_of((group * ndp + dp) * height, height), height)
        total = None
        for s in range(per):
            row = m * per + s
            lanes = slice(cut * width, (cut + 1) * width)
            part = h[row, at, lanes].astype(f32) * d_acts[m][row : row + 1, lanes]
            total = part if total is None else total + part
        return total

    def send_y(m):
        arrive(feat_copies[m])
        d_feat = total_of(f_slots, m)
        d_pooled = scale[m] * (
            d_feat
            - jnp.mean(d_feat, axis=-1, keepdims=True)
            - feat[m] * jnp.mean(d_feat * feat[m], axis=-1, keepdims=True)
        )
        d_pools.append(d_pooled)
        d_acts.append(matmul(d_pooled, down_ref[m], 1, 0))
        for cut in range(cuts):
            c = m * cuts + cut
            for group in range(ngroup):
                y_send[c, group] = term(m, cut, group, 1 - d).astype(bf16)
            copy = pltpu.make_async_remote_copy(
                src_ref=y_send.at[c], dst_ref=y_recv.at[c], send_sem=y_ss.at[c], recv_sem=y_rs.at[c],
                device_id={"dp": 1 - d}, device_id_type=MESH,
            )
            copy.start()
            y_copies.append(copy)

    def send_z(m):
        for cut in range(cuts):
            c = m * cuts + cut
            y_copies[c].wait_recv()
            for k in range(1, ngroup):
                to = lax.rem(g + k, ngroup)
                z_send[c, k - 1] = (term(m, cut, to, d) + y_recv[c, to].astype(f32)).astype(bf16)
                copy = pltpu.make_async_remote_copy(
                    src_ref=z_send.at[c, k - 1], dst_ref=z_recv.at[c, k - 1],
                    send_sem=z_ss.at[c * (ngroup - 1) + k - 1], recv_sem=z_rs.at[c * (ngroup - 1) + k - 1],
                    device_id={"group": to}, device_id_type=MESH,
                )
                copy.start()
                z_copies.append(copy)
            lanes = slice(cut * width, (cut + 1) * width)
            gup_ref[m, :, lanes] = term(m, cut, g, d) + y_recv[c, g].astype(f32)

    img[...] = jnp.zeros_like(img)
    img[0:apd, :] = img_ref[...].astype(f32)
    image = normalize_rows(img[...])[0]
    e_slots[r] = matmul(image, iproj_ref[...], 1, 0)
    pl.semaphore_wait(barrier, nmp - 1 + nr - 1)
    e_copies = spread(e_slots, e_ss, e_rs, False)
    forward(0)
    arrive(e_copies)
    embed = e_slots[...].reshape(nr * 8, -1)
    square = jnp.sum(embed * embed, axis=-1, keepdims=True)
    sq_slots[me] = jnp.broadcast_to(square, sq_slots.shape[1:])
    sq_copies = spread(sq_slots, sq_ss, sq_rs, True)
    forward(1)
    arrive(sq_copies)
    square = sq_slots[0]
    for k in range(1, nmp):
        square = square + sq_slots[k]
    anchors = (embed * lax.rsqrt(square[:, :1] + unit_eps)).astype(bf16)
    table = jnp.concatenate([anchors, jnp.zeros((128 - nr * 8, anchors.shape[1]), bf16)], axis=0)
    score(0, table)
    forward(2)
    loss_slope(0, table)
    score(1, table)
    products(0)
    send_y(0)
    score(2, table)
    ga[r] = jnp.concatenate([act[0] + act[1] + act[2], feat[0] + feat[1] + feat[2]], axis=0).astype(bf16)
    a_copies = spread(ga, a_ss, a_rs, False)
    loss_slope(1, table)
    products(1)
    loss_slope(2, table)
    send_y(1)
    products(2)
    send_y(2)
    d_embed = d_embeds[0] + d_embeds[1] + d_embeds[2]
    wide = jnp.concatenate([d_embed, jnp.zeros((rows, ga.shape[2] - d_embed.shape[1]), f32)], axis=1)
    gb[r] = jnp.concatenate([d_pools[0] + d_pools[1] + d_pools[2], wide], axis=0).astype(bf16)
    b_copies = spread(gb, b_ss, b_rs, False)
    for m in range(nmod):
        send_z(m)

    arrive(a_copies)
    arrive(b_copies)
    all_a = ga[...].reshape(nr * 16, -1)
    all_b = gb[...].reshape(nr * 16, -1)
    mine = pl.ds(pl.multiple_of(r * height, height), height)
    lane = lax.broadcasted_iota(jnp.int32, (1, nr * 16), 1) % 16
    emb = gproj_ref.shape[2]
    gt[...] = all_b.astype(f32).T
    lhs = gt[mine, :]
    for m in range(nmod):
        keep = (lane >= m * per) & (lane < (m + 1) * per)
        gdown_ref[m] = matmul(jnp.where(keep, lhs, 0.0), all_a, 1, 0)
    gt[...] = all_a.astype(f32).T
    lhs = gt[mine, :]
    for m in range(nmod):
        keep = (lane >= 8 + m * per) & (lane < 8 + (m + 1) * per)
        gproj_ref[m] = matmul(jnp.where(keep, lhs, 0.0), all_b[:, :emb], 1, 0)

    for m in range(nmod):
        for cut in range(cuts):
            c = m * cuts + cut
            lanes = slice(cut * width, (cut + 1) * width)
            total = gup_ref[m, :, lanes]
            for k in range(1, ngroup):
                z_copies[c * (ngroup - 1) + k - 1].wait_recv()
                total = total + z_recv[c, k - 1].astype(f32)
            gup_ref[m, :, lanes] = total
    for copy in sent + y_copies + z_copies:
        copy.wait_send()


def kernel_body(mesh, image_feats, image_proj, tokens, counts, pairing, w_up, w_down, w_proj):
    ngroup, ndp, nmp = mesh.shape["group"], mesh.shape["dp"], mesh.shape["mp"]
    nr = ngroup * ndp
    nmod, per, patches, width = tokens.shape
    hidden, emb = w_up.shape[2], w_proj.shape[2]
    apd, img_width = image_feats.shape
    cuts = 2
    sizes = (ngroup, ndp, nmp, per, apd, cuts)
    height = width // nr
    f32, bf16 = jnp.float32, jnp.bfloat16
    vmem = pl.BlockSpec(memory_space=pltpu.VMEM)
    smem = pl.BlockSpec(memory_space=pltpu.SMEM)
    sem = pltpu.SemaphoreType.DMA
    return pl.pallas_call(
        functools.partial(step_kernel, sizes),
        in_specs=[smem] * 2 + [vmem] * 6,
        out_specs=[vmem] * 3,
        out_shape=[
            jax.ShapeDtypeStruct((nmod, height, hidden), f32),
            jax.ShapeDtypeStruct((nmod, height, hidden), f32),
            jax.ShapeDtypeStruct((nmod, height, emb), f32),
        ],
        scratch_shapes=[
            pltpu.VMEM((8, img_width), f32),
            pltpu.VMEM((nmod * per, patches, width), bf16),
            pltpu.VMEM((nmod * per, patches, hidden), bf16),
            pltpu.VMEM((nmod * per, width, hidden), bf16),
            pltpu.VMEM((nr, 8, emb), f32),
            pltpu.VMEM((nmp, nr * 8, 128), f32),
            pltpu.VMEM((nmod, nmp, 8, width), f32),
            pltpu.VMEM((nmod, nmp, 8, 128), f32),
            pltpu.VMEM((nmod, nmp, 8, width), f32),
            pltpu.VMEM((nr, 16, width), bf16),
            pltpu.VMEM((nr, 16, width), bf16),
            pltpu.VMEM((width, nr * 16), f32),
            pltpu.VMEM((nmod * cuts, ngroup, height, hidden // cuts), bf16),
            pltpu.VMEM((nmod * cuts, ngroup, height, hidden // cuts), bf16),
            pltpu.VMEM((nmod * cuts, ngroup - 1, height, hidden // cuts), bf16),
            pltpu.VMEM((nmod * cuts, ngroup - 1, height, hidden // cuts), bf16),
        ]
        + [sem((nr - 1,))] * 2
        + [sem((nmp - 1,))] * 2
        + [sem((nmod * (nmp - 1),))] * 6
        + [sem((nr - 1,))] * 4
        + [sem((nmod * cuts,))] * 2
        + [sem((nmod * cuts * (ngroup - 1),))] * 2,
        compiler_params=pltpu.CompilerParams(
            collective_id=0, has_side_effects=True, vmem_limit_bytes=44 << 20
        ),
        name="step",
    )(counts, pairing, image_feats, image_proj, tokens, w_up, w_down, w_proj)


def solution(mesh):
    in_specs = (
        P(("group", "dp"), None),
        P(None, "mp"),
        P(None, ("group", "dp"), None, None),
        P(None, ("group", "dp")),
        P(None, ("group", "dp")),
        P(None, None, "mp"),
        P(None, None, "mp"),
        P(None, None, "mp"),
    )
    out_specs = (
        P(None, ("group", "dp"), "mp"),
        P(None, ("group", "dp"), "mp"),
        P(None, ("group", "dp"), "mp"),
    )
    devices = mesh.shape["group"] * mesh.shape["dp"]
    fits = devices <= 8 and mesh.shape["dp"] == 2
    body = functools.partial(kernel_body, mesh) if fits else plain_body
    return jax.shard_map(body, mesh=mesh, in_specs=in_specs, out_specs=out_specs, check_vma=False)
```

```python
import functools

import jax
import jax.numpy as jnp
from jax import lax
from jax.experimental import pallas as pl
from jax.experimental.pallas import tpu as pltpu
from jax.sharding import PartitionSpec as P

MESH = pl.DeviceIdType.MESH
inverse_temp = 14.285714285714286
norm_eps = 1e-05
unit_eps = 1e-06
root_half = 0.7071067811865476
gauss_coef = 0.3989422804014327


def normalize_rows(values):
    centre = jnp.mean(values, axis=-1, keepdims=True)
    spread = jnp.mean(jnp.square(values - centre), axis=-1, keepdims=True)
    scale_inv = lax.rsqrt(spread + norm_eps)
    return ((values - centre) * scale_inv, scale_inv)


def gelu_value(values):
    return 0.5 * values * (1.0 + lax.erf(values * root_half))


def gelu_slope(values):
    return (
        0.5 * (1.0 + lax.erf(values * root_half))
        + values * jnp.exp(-0.5 * values * values) * gauss_coef
    )


def plain_body(image_feats, image_proj, tokens, counts, pairing, w_up, w_down, w_proj):
    image_normed = normalize_rows(image_feats.astype(jnp.float32))[0].astype(jnp.bfloat16)
    embed_cols = jnp.dot(image_normed, image_proj, preferred_element_type=jnp.float32)
    anchor_sq = lax.psum(jnp.sum(embed_cols * embed_cols, axis=-1), "mp")
    anchor_cols = (embed_cols * lax.rsqrt(anchor_sq + unit_eps)[:, None]).astype(jnp.bfloat16)
    num_samples = tokens.shape[1]
    num_patches = tokens.shape[2]
    feature_width = tokens.shape[3]
    positions = jnp.arange(num_patches, dtype=jnp.int32)
    inside = positions[None, None, :] < counts[:, :, None]
    weight = jnp.where(inside, 1.0 / counts[:, :, None].astype(jnp.float32), 0.0)
    mask_bf = inside.astype(jnp.bfloat16)
    normed_list = []
    pre_list = []
    pool_list = []
    partials = []
    for modality in range(3):
        normed = (
            normalize_rows(tokens[modality].astype(jnp.float32))[0]
            .astype(jnp.bfloat16)
            .reshape(-1, feature_width)
        )
        pre_act = jnp.dot(normed, w_up[modality], preferred_element_type=jnp.float32).reshape(
            num_samples, num_patches, -1
        )
        act_pool = jnp.einsum("sp,spf->sf", weight[modality], gelu_value(pre_act)).astype(
            jnp.bfloat16
        )
        partials.append(
            lax.dot_general(
                act_pool,
                w_down[modality],
                (((1,), (1,)), ((), ())),
                preferred_element_type=jnp.float32,
            )
        )
        normed_list.append(normed)
        pre_list.append(pre_act)
        pool_list.append(act_pool)
    token_pool = jnp.einsum(
        "msp,mspd->msd", mask_bf, tokens, preferred_element_type=jnp.float32
    ) / counts[:, :, None].astype(jnp.float32)
    pooled = token_pool + lax.psum(jnp.stack(partials), "mp")
    feat_norm, scale_inv = normalize_rows(pooled)
    feat = feat_norm.astype(jnp.bfloat16)
    embedded = jnp.einsum("msd,mde->mse", feat, w_proj, preferred_element_type=jnp.float32)
    embed_sq = lax.psum(jnp.sum(embedded * embedded, axis=-1), "mp")
    inv_norm = lax.rsqrt(embed_sq + unit_eps)[..., None]
    unit_rows = embedded * inv_norm
    queries = unit_rows.astype(jnp.bfloat16).reshape(3 * num_samples, -1)
    target_rows = pairing.reshape(-1)
    own_table = lax.all_gather(anchor_cols, ("group", "dp"), axis=0, tiled=True)
    part_logits = jnp.dot(queries, own_table.T, preferred_element_type=jnp.float32)
    logits = inverse_temp * lax.psum(part_logits, "mp")
    exp_logits = jnp.exp(logits)
    prob_bf = (exp_logits / jnp.sum(exp_logits, axis=-1, keepdims=True)).astype(jnp.bfloat16)
    weighted = jnp.dot(prob_bf, own_table, preferred_element_type=jnp.float32)
    target = jnp.take(own_table, target_rows, axis=0).astype(jnp.float32)
    d_unit = (inverse_temp * (weighted - target)).reshape(unit_rows.shape)
    unit_dots = lax.psum(jnp.sum(unit_rows * d_unit, axis=-1), "mp")
    d_embed = ((d_unit - unit_rows * unit_dots[..., None]) * inv_norm).astype(jnp.bfloat16)
    d_feat = lax.psum(
        jnp.einsum("mse,mde->msd", d_embed, w_proj, preferred_element_type=jnp.float32), "mp"
    )
    d_pooled = (
        scale_inv
        * (
            d_feat
            - jnp.mean(d_feat, axis=-1, keepdims=True)
            - feat_norm * jnp.mean(d_feat * feat_norm, axis=-1, keepdims=True)
        )
    ).astype(jnp.bfloat16)
    pool_stack = jnp.stack(pool_list)
    feat_all, dpool_all, act_all, dembed_all = (
        lax.all_gather(feat, ("group", "dp"), axis=1, tiled=True),
        lax.all_gather(d_pooled, ("group", "dp"), axis=1, tiled=True),
        lax.all_gather(pool_stack, ("group", "dp"), axis=1, tiled=True),
        lax.all_gather(d_embed, ("group", "dp"), axis=1, tiled=True),
    )
    row_count = feature_width // lax.axis_size(("group", "dp"))
    row_start = lax.axis_index(("group", "dp")) * row_count
    feat_rows = lax.dynamic_slice_in_dim(feat_all, row_start, row_count, 2)
    dpool_rows = lax.dynamic_slice_in_dim(dpool_all, row_start, row_count, 2)
    down_shards = jnp.einsum(
        "msd,msf->mdf", dpool_rows, act_all, preferred_element_type=jnp.float32
    )
    proj_shards = jnp.einsum(
        "msd,mse->mde", feat_rows, dembed_all, preferred_element_type=jnp.float32
    )
    joined_list = []
    for modality in range(3):
        d_act = jnp.dot(d_pooled[modality], w_down[modality], preferred_element_type=jnp.float32)
        d_pre = (
            weight[modality][:, :, None] * d_act[:, None, :] * gelu_slope(pre_list[modality])
        ).astype(jnp.bfloat16)
        grad_up = lax.dot_general(
            normed_list[modality],
            d_pre.reshape(-1, d_pre.shape[2]),
            (((0,), (0,)), ((), ())),
            preferred_element_type=jnp.float32,
        )
        joined_list.append(grad_up)
    stacked = jnp.stack(joined_list)
    stacked = lax.psum_scatter(stacked, ("group", "dp"), scatter_dimension=1, tiled=True)
    return (stacked, down_shards, proj_shards)

def peer_of(r, ndp):
    return {"group": r // ndp, "dp": lax.rem(r, ndp)}


def step_kernel(
    sizes, count_ref, pair_ref, img_ref, iproj_ref, tok_ref, up_hbm, down_hbm, proj_hbm,
    gup_ref, gdown_ref, gproj_ref,
    up_ref, down_ref, proj_ref, w_sem, img, normed_of, sloped_of, h, e_slots, sq_slots, p_slots, l_slots, f_slots, ga, gb, gt,
    y_send, y_recv, z_send, z_recv, x_send, x_recv,
    e_ss, e_rs, sq_ss, sq_rs, p_ss, p_rs, l_ss, l_rs, f_ss, f_rs, a_ss, a_rs, b_ss, b_rs,
    y_ss, y_rs, z_ss, z_rs, x_ss, x_rs,
):
    ngroup, ndp, nmp, per, apd, cuts = sizes
    nr = ngroup * ndp
    g, d = lax.axis_index("group"), lax.axis_index("dp")
    r = g * ndp + d
    me = lax.axis_index("mp")
    nmod = down_ref.shape[0]
    rows = 8
    f32, bf16 = jnp.float32, jnp.bfloat16
    loads = {}
    for m in range(nmod):
        for i, (src, dst) in enumerate(((up_hbm, up_ref), (down_hbm, down_ref), (proj_hbm, proj_ref))):
            loads[i, m] = pltpu.make_async_copy(src.at[m], dst.at[m], w_sem.at[i * nmod + m])
            loads[i, m].start()
    barrier = pltpu.get_barrier_semaphore()
    for k in range(1, nmp):
        pl.semaphore_signal(barrier, inc=1, device_id={"mp": lax.rem(me + k, nmp)}, device_id_type=MESH)
    for k in range(1, nr):
        pl.semaphore_signal(barrier, inc=1, device_id=peer_of(lax.rem(r + k, nr), ndp), device_id_type=MESH)

    sent = []

    def spread(slots, ss, rs, across_mp, base=0, lead=()):
        slot = me if across_mp else r
        out = []
        for k in range(1, nmp if across_mp else nr):
            device = {"mp": lax.rem(me + k, nmp)} if across_mp else peer_of(lax.rem(r + k, nr), ndp)
            ref = slots.at[lead + (slot,)]
            copy = pltpu.make_async_remote_copy(
                src_ref=ref, dst_ref=ref, send_sem=ss.at[base + k - 1], recv_sem=rs.at[base + k - 1],
                device_id=device, device_id_type=MESH,
            )
            copy.start()
            out.append(copy)
        sent.extend(out)
        return out

    def arrive(copies):
        for copy in copies:
            copy.wait_recv()

    row_id = lax.broadcasted_iota(jnp.int32, (rows, 1), 0)
    col = lax.broadcasted_iota(jnp.int32, (rows, 128), 1)
    anchor_of = (col // 8) * apd + col % 8
    valid = (col % 8 < apd) & (col < nr * 8)

    def matmul(lhs, rhs, left, right):
        return lax.dot_general(
            lhs.astype(bf16), rhs, (((left,), (right,)), ((), ())), preferred_element_type=f32
        )

    act, pool, pooled_copies = [], [], []

    def forward(m):
        loads[0, m].wait()
        act_rows = jnp.zeros((rows, up_ref.shape[2]), f32)
        pool_rows = jnp.zeros((rows, tok_ref.shape[3]), f32)
        for s in range(per):
            row = m * per + s
            x = tok_ref[m, s].astype(f32)
            normed = normalize_rows(x)[0].astype(bf16)
            normed_of[row] = normed
            count = jnp.full((x.shape[0], 1), count_ref[s, m], jnp.int32)
            index = lax.broadcasted_iota(jnp.int32, (x.shape[0], 1), 0)
            weight = jnp.where(index < count, 1.0 / count.astype(f32), 0.0)
            pre = jnp.dot(normed, up_ref[m], preferred_element_type=f32)
            phi = 0.5 * (1.0 + lax.erf(pre * root_half))
            slope = phi + pre * jnp.exp(-0.5 * pre * pre) * gauss_coef
            sloped_of[row] = (weight * slope).astype(bf16)
            here = row_id == row
            act_rows = jnp.where(here, jnp.sum(weight * (pre * phi), axis=0, keepdims=True), act_rows)
            pool_rows = jnp.where(here, jnp.sum(weight * x, axis=0, keepdims=True), pool_rows)
        act_rows = act_rows.astype(bf16).astype(f32)
        act.append(act_rows)
        pool.append(pool_rows)
        loads[1, m].wait()
        p_slots[m, me] = matmul(act_rows, down_ref[m], 1, 1)
        pooled_copies.append(spread(p_slots, p_ss, p_rs, True, m * (nmp - 1), (m,)))

    feat, scale, embeds, logit_copies = [], [], [], []

    def total_of(slots, m):
        total = slots[m, 0]
        for k in range(1, nmp):
            total = total + slots[m, k]
        return total

    def score(m, table):
        arrive(pooled_copies[m])
        feat_norm, scale_inv = normalize_rows(pool[m] + total_of(p_slots, m))
        feat.append(feat_norm)
        scale.append(scale_inv)
        loads[2, m].wait()
        embedded = matmul(feat_norm, proj_ref[m], 1, 0)
        embeds.append(embedded)
        own_sq = jnp.sum(embedded * embedded, axis=-1, keepdims=True)
        part = matmul(embedded, table, 1, 1)
        l_slots[m, me] = jnp.where(col < nr * 8, part, own_sq)
        logit_copies.append(spread(l_slots, l_ss, l_rs, True, m * (nmp - 1), (m,)))

    d_embeds, feat_copies = [], []

    def loss_slope(m, table):
        hot = jnp.zeros((rows, 128), f32)
        for s in range(per):
            hot = jnp.where(valid & (anchor_of == pair_ref[s, m]) & (row_id == m * per + s), 1.0, hot)
        arrive(logit_copies[m])
        both = total_of(l_slots, m)
        inv_norm = lax.rsqrt(both[:, 127:] + unit_eps)
        logits = jnp.where(valid, inverse_temp * (both * inv_norm), 0.0)
        expl = jnp.where(valid, jnp.exp(logits), 0.0)
        prob = (expl / jnp.sum(expl, axis=-1, keepdims=True)).astype(bf16)
        dots = jnp.sum((prob.astype(f32) - hot) * logits, axis=-1, keepdims=True)
        d_unit = inverse_temp * (matmul(prob, table, 1, 0) - matmul(hot, table, 1, 0))
        d_embed = (d_unit - embeds[m] * inv_norm * dots) * inv_norm
        own = (row_id >= m * per) & (row_id < (m + 1) * per)
        d_embed = jnp.where(own, d_embed, 0.0).astype(bf16).astype(f32)
        d_embeds.append(d_embed)
        f_slots[m, me] = matmul(d_embed, proj_ref[m], 1, 1)
        feat_copies.append(spread(f_slots, f_ss, f_rs, True, m * (nmp - 1), (m,)))

    def products(m):
        for s in range(per):
            row = m * per + s
            h[row] = lax.dot_general(
                normed_of[row], sloped_of[row], (((0,), (0,)), ((), ())), preferred_element_type=f32
            ).astype(bf16)

    d_pools, d_acts, y_copies = [], [], []
    height, hidden = gup_ref.shape[1:]
    width = hidden // cuts

    def term(m, cut, group, dp):
        at = pl.ds(pl.multiple_of((group * ndp + dp) * height, height), height)
        total = None
        for s in range(per):
            row = m * per + s
            lanes = slice(cut * width, (cut + 1) * width)
            part = h[row, at, lanes].astype(f32) * d_acts[m][row : row + 1, lanes]
            total = part if total is None else total + part
        return total

    def send_y(m):
        arrive(feat_copies[m])
        d_feat = total_of(f_slots, m)
        d_pooled = scale[m] * (
            d_feat
            - jnp.mean(d_feat, axis=-1, keepdims=True)
            - feat[m] * jnp.mean(d_feat * feat[m], axis=-1, keepdims=True)
        )
        d_pools.append(d_pooled)
        d_acts.append(matmul(d_pooled, down_ref[m], 1, 0))
        for cut in range(cuts):
            c = m * cuts + cut
            for group in range(ngroup):
                y_send[c, group] = term(m, cut, group, 1 - d).astype(bf16)
            copy = pltpu.make_async_remote_copy(
                src_ref=y_send.at[c], dst_ref=y_recv.at[c], send_sem=y_ss.at[c], recv_sem=y_rs.at[c],
                device_id={"dp": 1 - d}, device_id_type=MESH,
            )
            copy.start()
            y_copies.append(copy)

    partner = g + 1 - 2 * lax.rem(g, 2)
    mirror = ngroup - 1 - g
    mirror_partner = ngroup - 1 - partner
    is_end = (g == 0) | (g == ngroup - 1)
    is_middle = jnp.logical_not(is_end)
    chunks = nmod * cuts

    def z_copy(c, blocks):
        return pltpu.make_async_remote_copy(
            src_ref=z_send.at[c, pl.ds(0, blocks)], dst_ref=z_recv.at[c, pl.ds(0, blocks)],
            send_sem=z_ss.at[c], recv_sem=z_rs.at[c],
            device_id={"group": partner}, device_id_type=MESH,
        )

    def x_copy(c, i, to):
        return pltpu.make_async_remote_copy(
            src_ref=x_send.at[c, i], dst_ref=x_recv.at[c],
            send_sem=x_ss.at[2 * c + i], recv_sem=x_rs.at[c],
            device_id={"group": to}, device_id_type=MESH,
        )

    def lanes_of(c):
        return slice((c % cuts) * width, (c % cuts + 1) * width)

    def summed(c, group):
        return term(c // cuts, c % cuts, group, d) + y_recv[c, group].astype(f32)

    def send_pair(c):
        y_copies[c].wait_recv()
        z_send[c, 0] = summed(c, partner).astype(bf16)

        @pl.when(is_end)
        def _():
            z_send[c, 1] = summed(c, mirror_partner).astype(bf16)
            z_send[c, 2] = summed(c, mirror).astype(bf16)
            z_copy(c, 3).start()

        @pl.when(is_middle)
        def _():
            z_copy(c, 1).start()

        gup_ref[c // cuts, :, lanes_of(c)] = summed(c, g)

    def send_across(c):
        @pl.when(is_middle)
        def _():
            z_copy(c, 3).wait_recv()
            x_send[c, 1] = (summed(c, mirror_partner) + z_recv[c, 2].astype(f32)).astype(bf16)
            x_copy(c, 1, mirror_partner).start()
            x_send[c, 0] = (summed(c, mirror) + z_recv[c, 1].astype(f32)).astype(bf16)
            x_copy(c, 0, mirror).start()

        @pl.when(is_end)
        def _():
            z_copy(c, 1).wait_recv()

    def finish(c):
        x_copy(c, 0, mirror).wait_recv()
        at = (c // cuts, slice(None), lanes_of(c))
        gup_ref[at] = gup_ref[at] + z_recv[c, 0].astype(f32) + x_recv[c].astype(f32)

        @pl.when(is_end)
        def _():
            z_copy(c, 3).wait_send()

        @pl.when(is_middle)
        def _():
            z_copy(c, 1).wait_send()
            x_copy(c, 0, mirror).wait_send()
            x_copy(c, 1, mirror_partner).wait_send()

    img[...] = jnp.zeros_like(img)
    img[0:apd, :] = img_ref[...].astype(f32)
    image = normalize_rows(img[...])[0]
    e_slots[r] = matmul(image, iproj_ref[...], 1, 0)
    pl.semaphore_wait(barrier, nmp - 1 + nr - 1)
    e_copies = spread(e_slots, e_ss, e_rs, False)
    forward(0)
    arrive(e_copies)
    embed = e_slots[...].reshape(nr * 8, -1)
    square = jnp.sum(embed * embed, axis=-1, keepdims=True)
    sq_slots[me] = jnp.broadcast_to(square, sq_slots.shape[1:])
    sq_copies = spread(sq_slots, sq_ss, sq_rs, True)
    forward(1)
    arrive(sq_copies)
    square = sq_slots[0]
    for k in range(1, nmp):
        square = square + sq_slots[k]
    anchors = (embed * lax.rsqrt(square[:, :1] + unit_eps)).astype(bf16)
    table = jnp.concatenate([anchors, jnp.zeros((128 - nr * 8, anchors.shape[1]), bf16)], axis=0)
    score(0, table)
    forward(2)
    loss_slope(0, table)
    score(1, table)
    products(0)
    send_y(0)
    score(2, table)
    ga[r] = jnp.concatenate([act[0] + act[1] + act[2], feat[0] + feat[1] + feat[2]], axis=0).astype(bf16)
    a_copies = spread(ga, a_ss, a_rs, False)
    loss_slope(1, table)
    products(1)
    loss_slope(2, table)
    send_y(1)
    send_pair(0)
    products(2)
    send_y(2)
    d_embed = d_embeds[0] + d_embeds[1] + d_embeds[2]
    wide = jnp.concatenate([d_embed, jnp.zeros((rows, ga.shape[2] - d_embed.shape[1]), f32)], axis=1)
    gb[r] = jnp.concatenate([d_pools[0] + d_pools[1] + d_pools[2], wide], axis=0).astype(bf16)
    b_copies = spread(gb, b_ss, b_rs, False)
    for c in range(1, chunks):
        send_pair(c)
        send_across(c - 1)
    send_across(chunks - 1)

    arrive(a_copies)
    arrive(b_copies)
    all_a = ga[...].reshape(nr * 16, -1)
    all_b = gb[...].reshape(nr * 16, -1)
    mine = pl.ds(pl.multiple_of(r * height, height), height)
    lane = lax.broadcasted_iota(jnp.int32, (1, nr * 16), 1) % 16
    emb = gproj_ref.shape[2]
    gt[...] = all_b.astype(f32).T
    lhs = gt[mine, :]
    for m in range(nmod):
        keep = (lane >= m * per) & (lane < (m + 1) * per)
        gdown_ref[m] = matmul(jnp.where(keep, lhs, 0.0), all_a, 1, 0)
    gt[...] = all_a.astype(f32).T
    lhs = gt[mine, :]
    for m in range(nmod):
        keep = (lane >= 8 + m * per) & (lane < 8 + (m + 1) * per)
        gproj_ref[m] = matmul(jnp.where(keep, lhs, 0.0), all_b[:, :emb], 1, 0)

    for c in range(chunks):
        finish(c)
    for copy in sent + y_copies:
        copy.wait_send()


def kernel_body(mesh, image_feats, image_proj, tokens, counts, pairing, w_up, w_down, w_proj):
    ngroup, ndp, nmp = mesh.shape["group"], mesh.shape["dp"], mesh.shape["mp"]
    nr = ngroup * ndp
    nmod, per, patches, width = tokens.shape
    hidden, emb = w_up.shape[2], w_proj.shape[2]
    apd, img_width = image_feats.shape
    cuts = 2
    sizes = (ngroup, ndp, nmp, per, apd, cuts)
    height = width // nr
    f32, bf16 = jnp.float32, jnp.bfloat16
    vmem = pl.BlockSpec(memory_space=pltpu.VMEM)
    smem = pl.BlockSpec(memory_space=pltpu.SMEM)
    sem = pltpu.SemaphoreType.DMA
    return pl.pallas_call(
        functools.partial(step_kernel, sizes),
        in_specs=[smem] * 2 + [vmem] * 3 + [pl.BlockSpec(memory_space=pl.ANY)] * 3,
        out_specs=[vmem] * 3,
        out_shape=[
            jax.ShapeDtypeStruct((nmod, height, hidden), f32),
            jax.ShapeDtypeStruct((nmod, height, hidden), f32),
            jax.ShapeDtypeStruct((nmod, height, emb), f32),
        ],
        scratch_shapes=[
            pltpu.VMEM(w_up.shape, bf16),
            pltpu.VMEM(w_down.shape, bf16),
            pltpu.VMEM(w_proj.shape, bf16),
            sem((3 * nmod,)),
            pltpu.VMEM((8, img_width), f32),
            pltpu.VMEM((nmod * per, patches, width), bf16),
            pltpu.VMEM((nmod * per, patches, hidden), bf16),
            pltpu.VMEM((nmod * per, width, hidden), bf16),
            pltpu.VMEM((nr, 8, emb), f32),
            pltpu.VMEM((nmp, nr * 8, 128), f32),
            pltpu.VMEM((nmod, nmp, 8, width), f32),
            pltpu.VMEM((nmod, nmp, 8, 128), f32),
            pltpu.VMEM((nmod, nmp, 8, width), f32),
            pltpu.VMEM((nr, 16, width), bf16),
            pltpu.VMEM((nr, 16, width), bf16),
            pltpu.VMEM((width, nr * 16), f32),
            pltpu.VMEM((nmod * cuts, ngroup, height, hidden // cuts), bf16),
            pltpu.VMEM((nmod * cuts, ngroup, height, hidden // cuts), bf16),
            pltpu.VMEM((nmod * cuts, 3, height, hidden // cuts), bf16),
            pltpu.VMEM((nmod * cuts, 3, height, hidden // cuts), bf16),
            pltpu.VMEM((nmod * cuts, 2, height, hidden // cuts), bf16),
            pltpu.VMEM((nmod * cuts, height, hidden // cuts), bf16),
        ]
        + [sem((nr - 1,))] * 2
        + [sem((nmp - 1,))] * 2
        + [sem((nmod * (nmp - 1),))] * 6
        + [sem((nr - 1,))] * 4
        + [sem((nmod * cuts,))] * 4
        + [sem((2 * nmod * cuts,)), sem((nmod * cuts,))],
        compiler_params=pltpu.CompilerParams(
            collective_id=0, has_side_effects=True, vmem_limit_bytes=51 << 20
        ),
        name="step",
    )(counts.T, pairing.T, image_feats, image_proj, tokens, w_up, w_down, w_proj)


def solution(mesh):
    in_specs = (
        P(("group", "dp"), None),
        P(None, "mp"),
        P(None, ("group", "dp"), None, None),
        P(None, ("group", "dp")),
        P(None, ("group", "dp")),
        P(None, None, "mp"),
        P(None, None, "mp"),
        P(None, None, "mp"),
    )
    out_specs = (
        P(None, ("group", "dp"), "mp"),
        P(None, ("group", "dp"), "mp"),
        P(None, ("group", "dp"), "mp"),
    )
    devices = mesh.shape["group"] * mesh.shape["dp"]
    fits = devices <= 8 and mesh.shape["dp"] == 2 and mesh.shape["group"] == 4
    body = functools.partial(kernel_body, mesh) if fits else plain_body
    return jax.shard_map(body, mesh=mesh, in_specs=in_specs, out_specs=out_specs, check_vma=False)
```

```python
import functools

import jax
import jax.numpy as jnp
from jax import lax
from jax.experimental import pallas as pl
from jax.experimental.pallas import tpu as pltpu
from jax.sharding import PartitionSpec as P

MESH = pl.DeviceIdType.MESH
inverse_temp = 14.285714285714286
norm_eps = 1e-05
unit_eps = 1e-06
root_half = 0.7071067811865476
gauss_coef = 0.3989422804014327


def normalize_rows(values):
    centre = jnp.mean(values, axis=-1, keepdims=True)
    spread = jnp.mean(jnp.square(values - centre), axis=-1, keepdims=True)
    scale_inv = lax.rsqrt(spread + norm_eps)
    return ((values - centre) * scale_inv, scale_inv)


def gelu_value(values):
    return 0.5 * values * (1.0 + lax.erf(values * root_half))


def gelu_slope(values):
    return (
        0.5 * (1.0 + lax.erf(values * root_half))
        + values * jnp.exp(-0.5 * values * values) * gauss_coef
    )


def plain_body(image_feats, image_proj, tokens, counts, pairing, w_up, w_down, w_proj):
    image_normed = normalize_rows(image_feats.astype(jnp.float32))[0].astype(jnp.bfloat16)
    embed_cols = jnp.dot(image_normed, image_proj, preferred_element_type=jnp.float32)
    anchor_sq = lax.psum(jnp.sum(embed_cols * embed_cols, axis=-1), "mp")
    anchor_cols = (embed_cols * lax.rsqrt(anchor_sq + unit_eps)[:, None]).astype(jnp.bfloat16)
    num_samples = tokens.shape[1]
    num_patches = tokens.shape[2]
    feature_width = tokens.shape[3]
    positions = jnp.arange(num_patches, dtype=jnp.int32)
    inside = positions[None, None, :] < counts[:, :, None]
    weight = jnp.where(inside, 1.0 / counts[:, :, None].astype(jnp.float32), 0.0)
    mask_bf = inside.astype(jnp.bfloat16)
    normed_list = []
    pre_list = []
    pool_list = []
    partials = []
    for modality in range(3):
        normed = (
            normalize_rows(tokens[modality].astype(jnp.float32))[0]
            .astype(jnp.bfloat16)
            .reshape(-1, feature_width)
        )
        pre_act = jnp.dot(normed, w_up[modality], preferred_element_type=jnp.float32).reshape(
            num_samples, num_patches, -1
        )
        act_pool = jnp.einsum("sp,spf->sf", weight[modality], gelu_value(pre_act)).astype(
            jnp.bfloat16
        )
        partials.append(
            lax.dot_general(
                act_pool,
                w_down[modality],
                (((1,), (1,)), ((), ())),
                preferred_element_type=jnp.float32,
            )
        )
        normed_list.append(normed)
        pre_list.append(pre_act)
        pool_list.append(act_pool)
    token_pool = jnp.einsum(
        "msp,mspd->msd", mask_bf, tokens, preferred_element_type=jnp.float32
    ) / counts[:, :, None].astype(jnp.float32)
    pooled = token_pool + lax.psum(jnp.stack(partials), "mp")
    feat_norm, scale_inv = normalize_rows(pooled)
    feat = feat_norm.astype(jnp.bfloat16)
    embedded = jnp.einsum("msd,mde->mse", feat, w_proj, preferred_element_type=jnp.float32)
    embed_sq = lax.psum(jnp.sum(embedded * embedded, axis=-1), "mp")
    inv_norm = lax.rsqrt(embed_sq + unit_eps)[..., None]
    unit_rows = embedded * inv_norm
    queries = unit_rows.astype(jnp.bfloat16).reshape(3 * num_samples, -1)
    target_rows = pairing.reshape(-1)
    own_table = lax.all_gather(anchor_cols, ("group", "dp"), axis=0, tiled=True)
    part_logits = jnp.dot(queries, own_table.T, preferred_element_type=jnp.float32)
    logits = inverse_temp * lax.psum(part_logits, "mp")
    exp_logits = jnp.exp(logits)
    prob_bf = (exp_logits / jnp.sum(exp_logits, axis=-1, keepdims=True)).astype(jnp.bfloat16)
    weighted = jnp.dot(prob_bf, own_table, preferred_element_type=jnp.float32)
    target = jnp.take(own_table, target_rows, axis=0).astype(jnp.float32)
    d_unit = (inverse_temp * (weighted - target)).reshape(unit_rows.shape)
    unit_dots = lax.psum(jnp.sum(unit_rows * d_unit, axis=-1), "mp")
    d_embed = ((d_unit - unit_rows * unit_dots[..., None]) * inv_norm).astype(jnp.bfloat16)
    d_feat = lax.psum(
        jnp.einsum("mse,mde->msd", d_embed, w_proj, preferred_element_type=jnp.float32), "mp"
    )
    d_pooled = (
        scale_inv
        * (
            d_feat
            - jnp.mean(d_feat, axis=-1, keepdims=True)
            - feat_norm * jnp.mean(d_feat * feat_norm, axis=-1, keepdims=True)
        )
    ).astype(jnp.bfloat16)
    pool_stack = jnp.stack(pool_list)
    feat_all, dpool_all, act_all, dembed_all = (
        lax.all_gather(feat, ("group", "dp"), axis=1, tiled=True),
        lax.all_gather(d_pooled, ("group", "dp"), axis=1, tiled=True),
        lax.all_gather(pool_stack, ("group", "dp"), axis=1, tiled=True),
        lax.all_gather(d_embed, ("group", "dp"), axis=1, tiled=True),
    )
    row_count = feature_width // lax.axis_size(("group", "dp"))
    row_start = lax.axis_index(("group", "dp")) * row_count
    feat_rows = lax.dynamic_slice_in_dim(feat_all, row_start, row_count, 2)
    dpool_rows = lax.dynamic_slice_in_dim(dpool_all, row_start, row_count, 2)
    down_shards = jnp.einsum(
        "msd,msf->mdf", dpool_rows, act_all, preferred_element_type=jnp.float32
    )
    proj_shards = jnp.einsum(
        "msd,mse->mde", feat_rows, dembed_all, preferred_element_type=jnp.float32
    )
    joined_list = []
    for modality in range(3):
        d_act = jnp.dot(d_pooled[modality], w_down[modality], preferred_element_type=jnp.float32)
        d_pre = (
            weight[modality][:, :, None] * d_act[:, None, :] * gelu_slope(pre_list[modality])
        ).astype(jnp.bfloat16)
        grad_up = lax.dot_general(
            normed_list[modality],
            d_pre.reshape(-1, d_pre.shape[2]),
            (((0,), (0,)), ((), ())),
            preferred_element_type=jnp.float32,
        )
        joined_list.append(grad_up)
    stacked = jnp.stack(joined_list)
    stacked = lax.psum_scatter(stacked, ("group", "dp"), scatter_dimension=1, tiled=True)
    return (stacked, down_shards, proj_shards)

def peer_of(r, ndp):
    return {"group": r // ndp, "dp": lax.rem(r, ndp)}


def step_kernel(
    sizes, count_ref, pair_ref, img_ref, iproj_ref, tok_ref, up_hbm, down_hbm, proj_hbm,
    gup_ref, gdown_ref, gproj_ref,
    up_ref, down_ref, proj_ref, w_sem, img, normed_of, sloped_of, h, e_slots, sq_slots, p_slots, l_slots, f_slots, ga, gb, gt,
    y_send, y_recv, z_send, z_recv, x_send, x_recv,
    e_ss, e_rs, sq_ss, sq_rs, p_ss, p_rs, l_ss, l_rs, f_ss, f_rs, a_ss, a_rs, b_ss, b_rs,
    y_ss, y_rs, z_ss, z_rs, x_ss, x_rs,
):
    ngroup, ndp, nmp, per, apd, cuts = sizes
    nr = ngroup * ndp
    g, d = lax.axis_index("group"), lax.axis_index("dp")
    r = g * ndp + d
    me = lax.axis_index("mp")
    nmod = down_ref.shape[0]
    rows = 8
    f32, bf16 = jnp.float32, jnp.bfloat16
    loads = {}
    for m in range(nmod):
        for i, (src, dst) in enumerate(((up_hbm, up_ref), (down_hbm, down_ref), (proj_hbm, proj_ref))):
            loads[i, m] = pltpu.make_async_copy(src.at[m], dst.at[m], w_sem.at[i * nmod + m])
            loads[i, m].start()
    barrier = pltpu.get_barrier_semaphore()
    for k in range(1, nmp):
        pl.semaphore_signal(barrier, inc=1, device_id={"mp": lax.rem(me + k, nmp)}, device_id_type=MESH)
    for k in range(1, nr):
        pl.semaphore_signal(barrier, inc=1, device_id=peer_of(lax.rem(r + k, nr), ndp), device_id_type=MESH)

    sent = []

    def spread(slots, ss, rs, across_mp, base=0, lead=()):
        slot = me if across_mp else r
        out = []
        for k in range(1, nmp if across_mp else nr):
            device = {"mp": lax.rem(me + k, nmp)} if across_mp else peer_of(lax.rem(r + k, nr), ndp)
            ref = slots.at[lead + (slot,)]
            copy = pltpu.make_async_remote_copy(
                src_ref=ref, dst_ref=ref, send_sem=ss.at[base + k - 1], recv_sem=rs.at[base + k - 1],
                device_id=device, device_id_type=MESH,
            )
            copy.start()
            out.append(copy)
        sent.extend(out)
        return out

    def arrive(copies):
        for copy in copies:
            copy.wait_recv()

    def gather_y(slots, ss, rs):
        copy = pltpu.make_async_remote_copy(
            src_ref=slots.at[r], dst_ref=slots.at[r], send_sem=ss.at[0], recv_sem=rs.at[0],
            device_id={"dp": 1 - d}, device_id_type=MESH,
        )
        copy.start()
        sent.append(copy)
        return copy

    def gather_z(slots, ss, rs):
        out = []
        ref = slots.at[pl.ds(g * ndp, ndp)]
        for k in range(1, ngroup):
            copy = pltpu.make_async_remote_copy(
                src_ref=ref, dst_ref=ref, send_sem=ss.at[k], recv_sem=rs.at[k],
                device_id={"group": lax.rem(g + k, ngroup)}, device_id_type=MESH,
            )
            copy.start()
            out.append(copy)
        sent.extend(out)
        return out

    row_id = lax.broadcasted_iota(jnp.int32, (rows, 1), 0)
    col = lax.broadcasted_iota(jnp.int32, (rows, 128), 1)
    anchor_of = (col // 8) * apd + col % 8
    valid = (col % 8 < apd) & (col < nr * 8)

    def matmul(lhs, rhs, left, right):
        return lax.dot_general(
            lhs.astype(bf16), rhs, (((left,), (right,)), ((), ())), preferred_element_type=f32
        )

    act, pool, pooled_copies = [], [], []

    def forward(m):
        loads[0, m].wait()
        act_rows = jnp.zeros((rows, up_ref.shape[2]), f32)
        pool_rows = jnp.zeros((rows, tok_ref.shape[3]), f32)
        for s in range(per):
            row = m * per + s
            x = tok_ref[m, s].astype(f32)
            normed = normalize_rows(x)[0].astype(bf16)
            normed_of[row] = normed
            count = jnp.full((x.shape[0], 1), count_ref[s, m], jnp.int32)
            index = lax.broadcasted_iota(jnp.int32, (x.shape[0], 1), 0)
            weight = jnp.where(index < count, 1.0 / count.astype(f32), 0.0)
            pre = jnp.dot(normed, up_ref[m], preferred_element_type=f32)
            phi = 0.5 * (1.0 + lax.erf(pre * root_half))
            slope = phi + pre * jnp.exp(-0.5 * pre * pre) * gauss_coef
            sloped_of[row] = (weight * slope).astype(bf16)
            here = row_id == row
            act_rows = jnp.where(here, jnp.sum(weight * (pre * phi), axis=0, keepdims=True), act_rows)
            pool_rows = jnp.where(here, jnp.sum(weight * x, axis=0, keepdims=True), pool_rows)
        act_rows = act_rows.astype(bf16).astype(f32)
        act.append(act_rows)
        pool.append(pool_rows)
        loads[1, m].wait()
        p_slots[m, me] = matmul(act_rows, down_ref[m], 1, 1)
        pooled_copies.append(spread(p_slots, p_ss, p_rs, True, m * (nmp - 1), (m,)))

    feat, scale, embeds, logit_copies = [], [], [], []

    def total_of(slots, m):
        total = slots[m, 0]
        for k in range(1, nmp):
            total = total + slots[m, k]
        return total

    def score(m, table):
        arrive(pooled_copies[m])
        feat_norm, scale_inv = normalize_rows(pool[m] + total_of(p_slots, m))
        feat.append(feat_norm)
        scale.append(scale_inv)
        loads[2, m].wait()
        embedded = matmul(feat_norm, proj_ref[m], 1, 0)
        embeds.append(embedded)
        own_sq = jnp.sum(embedded * embedded, axis=-1, keepdims=True)
        part = matmul(embedded, table, 1, 1)
        l_slots[m, me] = jnp.where(col < nr * 8, part, own_sq)
        logit_copies.append(spread(l_slots, l_ss, l_rs, True, m * (nmp - 1), (m,)))

    d_embeds, feat_copies = [], []

    def loss_slope(m, table):
        hot = jnp.zeros((rows, 128), f32)
        for s in range(per):
            hot = jnp.where(valid & (anchor_of == pair_ref[s, m]) & (row_id == m * per + s), 1.0, hot)
        arrive(logit_copies[m])
        both = total_of(l_slots, m)
        inv_norm = lax.rsqrt(both[:, 127:] + unit_eps)
        logits = jnp.where(valid, inverse_temp * (both * inv_norm), 0.0)
        expl = jnp.where(valid, jnp.exp(logits), 0.0)
        prob = (expl / jnp.sum(expl, axis=-1, keepdims=True)).astype(bf16)
        dots = jnp.sum((prob.astype(f32) - hot) * logits, axis=-1, keepdims=True)
        d_unit = inverse_temp * (matmul(prob, table, 1, 0) - matmul(hot, table, 1, 0))
        d_embed = (d_unit - embeds[m] * inv_norm * dots) * inv_norm
        own = (row_id >= m * per) & (row_id < (m + 1) * per)
        d_embed = jnp.where(own, d_embed, 0.0).astype(bf16).astype(f32)
        d_embeds.append(d_embed)
        f_slots[m, me] = matmul(d_embed, proj_ref[m], 1, 1)
        feat_copies.append(spread(f_slots, f_ss, f_rs, True, m * (nmp - 1), (m,)))

    def products(m):
        for s in range(per):
            row = m * per + s
            h[row] = lax.dot_general(
                normed_of[row], sloped_of[row], (((0,), (0,)), ((), ())), preferred_element_type=f32
            ).astype(bf16)

    d_pools, d_acts, y_copies = [], [], []
    height, hidden = gup_ref.shape[1:]
    width = hidden // cuts

    def term(m, cut, group, dp):
        at = pl.ds(pl.multiple_of((group * ndp + dp) * height, height), height)
        total = None
        for s in range(per):
            row = m * per + s
            lanes = slice(cut * width, (cut + 1) * width)
            part = h[row, at, lanes].astype(f32) * d_acts[m][row : row + 1, lanes]
            total = part if total is None else total + part
        return total

    def grad_act(m):
        arrive(feat_copies[m])
        d_feat = total_of(f_slots, m)
        d_pooled = scale[m] * (
            d_feat
            - jnp.mean(d_feat, axis=-1, keepdims=True)
            - feat[m] * jnp.mean(d_feat * feat[m], axis=-1, keepdims=True)
        )
        d_pools.append(d_pooled)
        d_acts.append(matmul(d_pooled, down_ref[m], 1, 0))

    def push_y(m):
        for cut in range(cuts):
            c = m * cuts + cut
            for group in range(ngroup):
                y_send[c, group] = term(m, cut, group, 1 - d).astype(bf16)
            copy = pltpu.make_async_remote_copy(
                src_ref=y_send.at[c], dst_ref=y_recv.at[c], send_sem=y_ss.at[c], recv_sem=y_rs.at[c],
                device_id={"dp": 1 - d}, device_id_type=MESH,
            )
            copy.start()
            y_copies.append(copy)

    partner = g + 1 - 2 * lax.rem(g, 2)
    mirror = ngroup - 1 - g
    mirror_partner = ngroup - 1 - partner
    is_end = (g == 0) | (g == ngroup - 1)
    is_middle = jnp.logical_not(is_end)
    chunks = nmod * cuts

    def z_copy(c, blocks):
        return pltpu.make_async_remote_copy(
            src_ref=z_send.at[c, pl.ds(0, blocks)], dst_ref=z_recv.at[c, pl.ds(0, blocks)],
            send_sem=z_ss.at[c], recv_sem=z_rs.at[c],
            device_id={"group": partner}, device_id_type=MESH,
        )

    def x_copy(c, i, to):
        return pltpu.make_async_remote_copy(
            src_ref=x_send.at[c, i], dst_ref=x_recv.at[c],
            send_sem=x_ss.at[2 * c + i], recv_sem=x_rs.at[c],
            device_id={"group": to}, device_id_type=MESH,
        )

    def lanes_of(c):
        return slice((c % cuts) * width, (c % cuts + 1) * width)

    def summed(c, group):
        return term(c // cuts, c % cuts, group, d) + y_recv[c, group].astype(f32)

    def send_pair(c):
        y_copies[c].wait_recv()
        z_send[c, 0] = summed(c, partner).astype(bf16)

        @pl.when(is_end)
        def _():
            z_send[c, 1] = summed(c, mirror_partner).astype(bf16)
            z_send[c, 2] = summed(c, mirror).astype(bf16)
            z_copy(c, 3).start()

        @pl.when(is_middle)
        def _():
            z_copy(c, 1).start()

        gup_ref[c // cuts, :, lanes_of(c)] = summed(c, g)

    def send_across(c):
        @pl.when(is_middle)
        def _():
            z_copy(c, 3).wait_recv()
            x_send[c, 1] = (summed(c, mirror_partner) + z_recv[c, 2].astype(f32)).astype(bf16)
            x_copy(c, 1, mirror_partner).start()
            x_send[c, 0] = (summed(c, mirror) + z_recv[c, 1].astype(f32)).astype(bf16)
            x_copy(c, 0, mirror).start()

        @pl.when(is_end)
        def _():
            z_copy(c, 1).wait_recv()

    def finish(c):
        x_copy(c, 0, mirror).wait_recv()
        at = (c // cuts, slice(None), lanes_of(c))
        gup_ref[at] = gup_ref[at] + z_recv[c, 0].astype(f32) + x_recv[c].astype(f32)

        @pl.when(is_end)
        def _():
            z_copy(c, 3).wait_send()

        @pl.when(is_middle)
        def _():
            z_copy(c, 1).wait_send()
            x_copy(c, 0, mirror).wait_send()
            x_copy(c, 1, mirror_partner).wait_send()

    img[...] = jnp.zeros_like(img)
    img[0:apd, :] = img_ref[...].astype(f32)
    image = normalize_rows(img[...])[0]
    e_slots[r] = matmul(image, iproj_ref[...], 1, 0)
    pl.semaphore_wait(barrier, nmp - 1 + nr - 1)
    e_copies = spread(e_slots, e_ss, e_rs, False)
    forward(0)
    arrive(e_copies)
    embed = e_slots[...].reshape(nr * 8, -1)
    square = jnp.sum(embed * embed, axis=-1, keepdims=True)
    sq_slots[me] = jnp.broadcast_to(square, sq_slots.shape[1:])
    sq_copies = spread(sq_slots, sq_ss, sq_rs, True)
    forward(1)
    arrive(sq_copies)
    square = sq_slots[0]
    for k in range(1, nmp):
        square = square + sq_slots[k]
    anchors = (embed * lax.rsqrt(square[:, :1] + unit_eps)).astype(bf16)
    table = jnp.concatenate([anchors, jnp.zeros((128 - nr * 8, anchors.shape[1]), bf16)], axis=0)
    score(0, table)
    forward(2)
    loss_slope(0, table)
    score(1, table)
    products(0)
    grad_act(0)
    push_y(0)
    score(2, table)
    ga[r] = jnp.concatenate([act[0] + act[1] + act[2], feat[0] + feat[1] + feat[2]], axis=0).astype(bf16)
    a_first = gather_y(ga, a_ss, a_rs)
    loss_slope(1, table)
    products(1)
    loss_slope(2, table)
    grad_act(1)
    push_y(1)
    send_pair(0)
    products(2)
    grad_act(2)
    d_embed = d_embeds[0] + d_embeds[1] + d_embeds[2]
    wide = jnp.concatenate([d_embed, jnp.zeros((rows, ga.shape[2] - d_embed.shape[1]), f32)], axis=1)
    gb[r] = jnp.concatenate([d_pools[0] + d_pools[1] + d_pools[2], wide], axis=0).astype(bf16)
    b_first = gather_y(gb, b_ss, b_rs)
    push_y(2)
    a_first.wait_recv()
    a_copies = gather_z(ga, a_ss, a_rs)
    for c in range(1, chunks):
        send_pair(c)
        send_across(c - 1)
    b_first.wait_recv()
    b_copies = gather_z(gb, b_ss, b_rs)
    send_across(chunks - 1)

    arrive(a_copies)
    arrive(b_copies)
    all_a = ga[...].reshape(nr * 16, -1)
    all_b = gb[...].reshape(nr * 16, -1)
    mine = pl.ds(pl.multiple_of(r * height, height), height)
    lane = lax.broadcasted_iota(jnp.int32, (1, nr * 16), 1) % 16
    emb = gproj_ref.shape[2]
    gt[...] = all_b.astype(f32).T
    lhs = gt[mine, :]
    for m in range(nmod):
        keep = (lane >= m * per) & (lane < (m + 1) * per)
        gdown_ref[m] = matmul(jnp.where(keep, lhs, 0.0), all_a, 1, 0)
    gt[...] = all_a.astype(f32).T
    lhs = gt[mine, :]
    for m in range(nmod):
        keep = (lane >= 8 + m * per) & (lane < 8 + (m + 1) * per)
        gproj_ref[m] = matmul(jnp.where(keep, lhs, 0.0), all_b[:, :emb], 1, 0)

    for c in range(chunks):
        finish(c)
    for copy in sent + y_copies:
        copy.wait_send()


def kernel_body(mesh, image_feats, image_proj, tokens, counts, pairing, w_up, w_down, w_proj):
    ngroup, ndp, nmp = mesh.shape["group"], mesh.shape["dp"], mesh.shape["mp"]
    nr = ngroup * ndp
    nmod, per, patches, width = tokens.shape
    hidden, emb = w_up.shape[2], w_proj.shape[2]
    apd, img_width = image_feats.shape
    cuts = 2
    sizes = (ngroup, ndp, nmp, per, apd, cuts)
    height = width // nr
    f32, bf16 = jnp.float32, jnp.bfloat16
    vmem = pl.BlockSpec(memory_space=pltpu.VMEM)
    smem = pl.BlockSpec(memory_space=pltpu.SMEM)
    sem = pltpu.SemaphoreType.DMA
    return pl.pallas_call(
        functools.partial(step_kernel, sizes),
        in_specs=[smem] * 2 + [vmem] * 3 + [pl.BlockSpec(memory_space=pl.ANY)] * 3,
        out_specs=[vmem] * 3,
        out_shape=[
            jax.ShapeDtypeStruct((nmod, height, hidden), f32),
            jax.ShapeDtypeStruct((nmod, height, hidden), f32),
            jax.ShapeDtypeStruct((nmod, height, emb), f32),
        ],
        scratch_shapes=[
            pltpu.VMEM(w_up.shape, bf16),
            pltpu.VMEM(w_down.shape, bf16),
            pltpu.VMEM(w_proj.shape, bf16),
            sem((3 * nmod,)),
            pltpu.VMEM((8, img_width), f32),
            pltpu.VMEM((nmod * per, patches, width), bf16),
            pltpu.VMEM((nmod * per, patches, hidden), bf16),
            pltpu.VMEM((nmod * per, width, hidden), bf16),
            pltpu.VMEM((nr, 8, emb), f32),
            pltpu.VMEM((nmp, nr * 8, 128), f32),
            pltpu.VMEM((nmod, nmp, 8, width), f32),
            pltpu.VMEM((nmod, nmp, 8, 128), f32),
            pltpu.VMEM((nmod, nmp, 8, width), f32),
            pltpu.VMEM((nr, 16, width), bf16),
            pltpu.VMEM((nr, 16, width), bf16),
            pltpu.VMEM((width, nr * 16), f32),
            pltpu.VMEM((nmod * cuts, ngroup, height, hidden // cuts), bf16),
            pltpu.VMEM((nmod * cuts, ngroup, height, hidden // cuts), bf16),
            pltpu.VMEM((nmod * cuts, 3, height, hidden // cuts), bf16),
            pltpu.VMEM((nmod * cuts, 3, height, hidden // cuts), bf16),
            pltpu.VMEM((nmod * cuts, 2, height, hidden // cuts), bf16),
            pltpu.VMEM((nmod * cuts, height, hidden // cuts), bf16),
        ]
        + [sem((nr - 1,))] * 2
        + [sem((nmp - 1,))] * 2
        + [sem((nmod * (nmp - 1),))] * 6
        + [sem((nr - 1,))] * 4
        + [sem((nmod * cuts,))] * 4
        + [sem((2 * nmod * cuts,)), sem((nmod * cuts,))],
        compiler_params=pltpu.CompilerParams(
            collective_id=0, has_side_effects=True, vmem_limit_bytes=46 << 20
        ),
        name="step",
    )(counts.T, pairing.T, image_feats, image_proj, tokens, w_up, w_down, w_proj)


def solution(mesh):
    in_specs = (
        P(("group", "dp"), None),
        P(None, "mp"),
        P(None, ("group", "dp"), None, None),
        P(None, ("group", "dp")),
        P(None, ("group", "dp")),
        P(None, None, "mp"),
        P(None, None, "mp"),
        P(None, None, "mp"),
    )
    out_specs = (
        P(None, ("group", "dp"), "mp"),
        P(None, ("group", "dp"), "mp"),
        P(None, ("group", "dp"), "mp"),
    )
    devices = mesh.shape["group"] * mesh.shape["dp"]
    fits = devices <= 8 and mesh.shape["dp"] == 2 and mesh.shape["group"] == 4
    body = functools.partial(kernel_body, mesh) if fits else plain_body
    return jax.shard_map(body, mesh=mesh, in_specs=in_specs, out_specs=out_specs, check_vma=False)
```
